256 devices in a mesh: rows: 32 (over z, x_lo, core), chan: 8 (over y, x_hi).
Axes of the slice: x: 4 (x_hi: 2, x_lo: 2; x = x_hi * 2 + x_lo), y: 4, z: 8, core: 2. Of those that a mesh axis runs over, the one named last changes fastest.
Arguments:
- feature: bfloat16 [96, 144, 1536], P('rows', None, 'chan'), may hold values from -6 to 6
- kernel: float32 [7, 7, 1536], P(None, None, 'chan'), may hold values from -0.875 to 0.875
- ln_gain: float32 [1536], replicated, may hold values from 0.1 to 1.9
- layer_scale: float32 [1536], replicated, may hold values from 0.1 to 1.9
- w_in: bfloat16 [1536, 6144], P(None, 'chan'), may hold values from -0.15625 to 0.15625
- w_out: bfloat16 [6144, 1536], P('chan'), may hold values from -0.078125 to 0.078125
- cotangent: bfloat16 [96, 144, 1536], P('rows'), may hold values from -6 to 6
Outputs:
- grad_feature: bfloat16 [96, 144, 1536], P('rows', None, 'chan')
- grad_w_in: float32 [1536, 6144], P('rows', 'chan')
- grad_w_out: float32 [6144, 1536], P('chan', 'rows')
- grad_kernel: float32 [7, 7, 1536], P(None, None, 'chan')
The draws below stay inside these ranges and needn't reach their ends.
All inputs are finite; a program needn't handle non-finite values.
Results may differ from the reference program's by a relative error of at most 0.03.
Values may be sent and summed in bfloat16 or wider, within the bound.
No kernel may reach another device: no remote copies, remote signals or barrier semaphores. Data moves between devices by JAX's collectives and lax.ppermute only.
A program may use at most 128 MiB of HBM per device.

```python
import math
import jax
import jax.numpy as jnp
from jax import lax

C = 1536
FF = 6144
KS = 7
ROWS_DEV = 3
COLS = 144
ROWS_ALL = 96
N_ROWS = 32


def spiked(entries, rng, source, target, blocks, factor):
    owner, partner = [(jnp.arange(entries.shape[position]) // (entries.shape[position] // blocks)).reshape([-1 if axis == position else 1 for axis in range(entries.ndim)]) for position in (source, target)]
    chosen = jax.random.permutation(rng, blocks)[partner]
    strong = (owner == chosen) | (owner == (partner + blocks // 2) % blocks)
    return jnp.where(strong, factor * entries, entries)


def block_scale(rng, shape, cuts, smallest, high):
    def one(position, shards_of):
        draws = jax.random.uniform(jax.random.fold_in(jax.random.fold_in(rng, 6), position), (shards_of,), jnp.float32, smallest / len(cuts), high / len(cuts))
        return jnp.repeat(jnp.exp(draws), shape[position] // shards_of).reshape((-1,) + (1,) * (len(shape) - position - 1))

    gain = one(*cuts[0])
    for cut in cuts[1:]:
        gain = gain * one(*cut)
    return gain


def bell_draw(own_key, dims, scale, limit, pieces=(), dtype=jnp.bfloat16):
    values = scale * jax.random.normal(own_key, dims, jnp.float32)
    if pieces:
        values = values * block_scale(own_key, dims, pieces, -0.22, 0.18)
    return jnp.clip(values, -limit, limit).astype(dtype)


def bell_draw_with(rng, extent, deviation, limit, pieces, heavy, dtype=jnp.bfloat16):
    values = deviation * jax.random.normal(rng, extent, jnp.float32)
    if pieces:
        values = values * block_scale(rng, extent, pieces, -0.22, 0.18)
    return jnp.clip(spiked(values, jax.random.fold_in(rng, 3), *heavy), -limit, limit).astype(dtype)


def setup_inputs(seed: int = 0) -> dict:
    streams_of = jax.random.split(jax.random.key(seed), 8)
    return {
        "feature": bell_draw(streams_of[0], (ROWS_ALL, COLS, C), 1.0, 6.0, ((0, 32), (2, 8))),
        "kernel": bell_draw(streams_of[1], (KS, KS, C), (KS * KS) ** -0.5, 0.875, ((2, 8),), jnp.float32),
        "ln_gain": jnp.clip(1.0 + 0.18 * jax.random.normal(streams_of[2], (C,), jnp.float32), 0.1, 1.9),
        "layer_scale": jnp.clip(1.0 + 0.18 * jax.random.normal(streams_of[3], (C,), jnp.float32), 0.1, 1.9),
        "w_in": bell_draw(streams_of[4], (C, FF), C ** -0.5, 0.15625, ((1, 8),)),
        "w_out": bell_draw(streams_of[5], (FF, C), FF ** -0.5, 0.078125, ((0, 8),)),
        "cotangent": bell_draw_with(streams_of[6], (ROWS_ALL, COLS, C), 1.0, 6.0, ((0, 32),), (0, 2, 32, 2.75)),
    }


def conv_taps(padded, kernel, height, width):
    result = jnp.zeros((height, width, kernel.shape[2]), jnp.float32)
    for tap_row in range(KS):
        for tap_col in range(KS):
            window = padded[tap_row:tap_row + height, tap_col:tap_col + width].astype(jnp.float32)
            result = result + window * kernel[tap_row, tap_col]
    return result

def conv_back(grad_pad, kernel, height, width):
    result = jnp.zeros((height, width, kernel.shape[2]), jnp.float32)
    for tap_row in range(KS):
        for tap_col in range(KS):
            window = grad_pad[6 - tap_row:6 - tap_row + height, 6 - tap_col:6 - tap_col + width].astype(jnp.float32)
            result = result + window * kernel[tap_row, tap_col]
    return result

def kernel_terms(grad_conv, padded, height, width):
    grad_float = grad_conv.astype(jnp.float32)
    rows_list = []
    for tap_row in range(KS):
        cols_list = []
        for tap_col in range(KS):
            window = padded[tap_row:tap_row + height, tap_col:tap_col + width].astype(jnp.float32)
            cols_list.append(lax.optimization_barrier(jnp.sum(grad_float * window, axis=(0, 1))))
        rows_list.append(jnp.stack(cols_list))
    return jnp.stack(rows_list)

def gelu_tanh(value):
    return jax.nn.gelu(value, approximate=True)

def reference(feature, kernel, ln_gain, layer_scale, w_in, w_out, cotangent):
    scale = 1.0 / math.sqrt(ROWS_ALL * COLS)
    padded = jnp.pad(feature, ((3, 3), (3, 3), (0, 0)))
    conv_out = conv_taps(padded, kernel, ROWS_ALL, COLS).astype(jnp.bfloat16)
    pixels = ROWS_DEV * COLS
    conv_blocks = conv_out.reshape(N_ROWS, pixels, C)
    cot_blocks = cotangent.reshape(N_ROWS, pixels, C)

    def block_step(carry, pair):
        conv_blk, cot_blk = pair
        values = conv_blk.astype(jnp.float32)
        mean = lax.optimization_barrier(jnp.mean(values, axis=1, keepdims=True))
        centred = values - mean
        var = lax.optimization_barrier(jnp.mean(centred * centred, axis=1, keepdims=True))
        rstd = 1.0 / jnp.sqrt(var + 1e-06)
        nhat = centred * rstd
        normed = (nhat * ln_gain).astype(jnp.bfloat16)
        hidden = jnp.dot(normed, w_in, preferred_element_type=jnp.float32)
        activ = gelu_tanh(hidden).astype(jnp.bfloat16)
        grad_mixed = (cot_blk.astype(jnp.float32) * layer_scale).astype(jnp.bfloat16)
        grad_activ = lax.dot_general(grad_mixed, w_out, (((1,), (1,)), ((), ())), preferred_element_type=jnp.float32)
        grad_hidden = jax.vjp(gelu_tanh, hidden)[1](grad_activ)[0].astype(jnp.bfloat16)
        part_out = lax.dot_general(activ, grad_mixed, (((0,), (0,)), ((), ())), preferred_element_type=jnp.float32)
        part_in = lax.dot_general(normed, grad_hidden, (((0,), (0,)), ((), ())), preferred_element_type=jnp.float32)
        grad_normed = lax.dot_general(grad_hidden, w_in, (((1,), (1,)), ((), ())), preferred_element_type=jnp.float32)
        scaled = grad_normed * ln_gain
        first_mean = lax.optimization_barrier(jnp.mean(scaled, axis=1, keepdims=True))
        second_mean = lax.optimization_barrier(jnp.mean(scaled * nhat, axis=1, keepdims=True))
        grad_conv = (rstd * (scaled - first_mean - nhat * second_mean)).astype(jnp.bfloat16)
        return ((carry[0] + part_in, carry[1] + part_out), grad_conv)
    start = (jnp.zeros((C, FF), jnp.float32), jnp.zeros((FF, C), jnp.float32))
    totals, grad_blocks = lax.scan(block_step, start, (conv_blocks, cot_blocks))
    grad_conv = grad_blocks.reshape(ROWS_ALL, COLS, C)
    grad_pad = jnp.pad(grad_conv, ((3, 3), (3, 3), (0, 0)))
    grad_feature = (cotangent.astype(jnp.float32) + conv_back(grad_pad, kernel, ROWS_ALL, COLS)).astype(jnp.bfloat16)
    grad_kernel = kernel_terms(grad_conv, padded, ROWS_ALL, COLS) * scale
    return (grad_feature, totals[0] * scale, totals[1] * scale, grad_kernel)
```

```python
import math

import jax
import jax.numpy as jnp
from jax import lax
from jax.experimental import pallas as pl
from jax.experimental.pallas import tpu as pltpu
from jax.sharding import PartitionSpec as P

F32 = jnp.float32
BF16 = jnp.bfloat16

ROWS = 3
COLS = 144
PIX = ROWS * COLS
HALF = COLS // 2
CH = 192
REM = ROWS * HALF
PACK = 656
MOM = 656
PAY = 704
GRP = 48
CALL = 1536
FF = 768
MAIN = 1024


def lanes(shape):
    return lax.broadcasted_iota(jnp.int32, shape, len(shape) - 1)


def swap(x):
    return pltpu.roll(x, 64, x.ndim - 1)


def limit(mib):
    return pltpu.CompilerParams(vmem_limit_bytes=mib * 1024 * 1024)


def pack_kernel(x_ref, o_ref):
    parts = []
    low = lanes((HALF, 128)) < 64
    for i in range(ROWS):
        row = x_ref[i].astype(F32)
        o_ref[i * COLS : (i + 1) * COLS, :] = row[:, :128].astype(BF16)
        rem = jnp.concatenate([row[:, 128:], row[:, 128:]], axis=1)
        parts.append(jnp.where(low, rem[:HALF], rem[HALF:]))
    parts.append(jnp.zeros((PACK - PIX - REM, 128), F32))
    o_ref[PIX:PACK, :] = jnp.concatenate(parts, axis=0).astype(BF16)


def fill_pads(blocks, main_pad, rem_pad):
    low = lanes((8, 128)) < 64
    for n, block in enumerate(blocks):
        main = block[:PIX, :].astype(F32)
        rem = block[PIX:PACK, :].astype(F32)
        for i in range(ROWS):
            r = n * ROWS + i
            main_pad[r, 0:8, :] = jnp.zeros((8, 128), F32)
            main_pad[r, 8 : 8 + COLS, :] = main[i * COLS : (i + 1) * COLS]
            main_pad[r, 8 + COLS : 16 + COLS, :] = jnp.zeros((8, 128), F32)
            part = rem[i * HALF : (i + 1) * HALF]
            rem_pad[r, 8 : 8 + HALF, :] = part
            rem_pad[r, 0:8, :] = jnp.where(low, 0.0, swap(part[HALF - 8 :]))
            rem_pad[r, 8 + HALF : 16 + HALF, :] = jnp.where(low, swap(part[:8]), 0.0)


def taps_block(pad, k_ref, lane0, start, count, flip):
    acc = [None] * ROWS
    for b in range(7):
        for r in range(9):
            window = pad[r, start + 5 + b : start + 5 + b + count, :]
            for i in range(ROWS):
                a = r - i
                if 0 <= a <= 6:
                    tap = (6 - a) * 7 + (6 - b) if flip else a * 7 + b
                    term = window * k_ref[tap : tap + 1, lane0 : lane0 + 128]
                    acc[i] = term if acc[i] is None else acc[i] + term
    return acc


def conv_kernel(top, own, bot, k_ref, o_ref, main_pad, rem_pad):
    fill_pads((top, own, bot), main_pad, rem_pad)
    for start in range(0, COLS, 48):
        acc = taps_block(main_pad, k_ref, 0, start, 48, False)
        for i in range(ROWS):
            o_ref[i * COLS + start : i * COLS + start + 48, :] = acc[i].astype(BF16)
    parts = [[] for _ in range(ROWS)]
    for start in range(0, HALF, 24):
        acc = taps_block(rem_pad, k_ref, 128, start, 24, False)
        for i in range(ROWS):
            parts[i].append(acc[i])
    flat = [p for row in parts for p in row] + [jnp.zeros((PACK - PIX - REM, 128), F32)]
    o_ref[PIX:PACK, :] = jnp.concatenate(flat, axis=0).astype(BF16)


def back_kernel(top, own, bot, k_ref, cot_ref, o_ref, main_pad, rem_pad):
    fill_pads((top, own, bot), main_pad, rem_pad)
    for start in range(0, COLS, 48):
        acc = taps_block(main_pad, k_ref, 0, start, 48, True)
        for i in range(ROWS):
            cot = cot_ref[i, start : start + 48, :128].astype(F32)
            o_ref[i, start : start + 48, :128] = (acc[i] + cot).astype(BF16)
    parts = [[] for _ in range(ROWS)]
    for start in range(0, HALF, 24):
        acc = taps_block(rem_pad, k_ref, 128, start, 24, True)
        for i in range(ROWS):
            parts[i].append(acc[i])
    for i in range(ROWS):
        rem = jnp.concatenate(parts[i], axis=0)
        both = jnp.concatenate([rem[:, :64], swap(rem)[:, :64]], axis=0)
        cot = cot_ref[i, :, 128:].astype(F32)
        o_ref[i, :, 128:] = (both + cot).astype(BF16)


def terms_kernel(scale, grad, top, own, bot, o_ref, main_pad, rem_pad):
    fill_pads((top, own, bot), main_pad, rem_pad)
    gmain = grad[:PIX, :].astype(F32)
    grem = grad[PIX:PACK, :].astype(F32)
    for pad, part, width, base, folded in (
        (main_pad, gmain, COLS, 0, False),
        (rem_pad, grem, HALF, 56, True),
    ):
        for b in range(7):
            acc = [jnp.zeros((8, 128), F32)] * 7
            for start in range(0, width, 8):
                windows = [pad[r, start + 5 + b : start + 13 + b, :] for r in range(9)]
                for i in range(ROWS):
                    g = part[i * width + start : i * width + start + 8]
                    for a in range(7):
                        acc[a] = acc[a] + g * windows[i + a]
            for a in range(7):
                total = jnp.sum(acc[a], axis=0, keepdims=True) * scale
                if folded:
                    total = total + swap(total)
                o_ref[base + a * 7 + b : base + a * 7 + b + 1, :] = total
    for base in (49, 105):
        o_ref[base : base + 7, :] = jnp.zeros((7, 128), F32)


def first_kernel(blk, cot, scale, w_out, w_in, mixed, activ_grad, w_slot):
    mixed[...] = (cot[...].astype(F32) * scale[...]).astype(BF16)
    activ_grad[...] = lax.dot_general(
        mixed[...], w_out[...], (((1,), (1,)), ((), ())), preferred_element_type=F32
    )
    for s in range(8):
        row = pl.multiple_of(blk[s] * CH, 64)
        w_slot[128 * s : 128 * s + 128, :] = w_in[pl.ds(row, 128), :]
        row = pl.multiple_of(blk[s] * CH + 128, 64)
        w_slot[MAIN + 64 * s : MAIN + 64 * s + 64, :] = w_in[pl.ds(row, 64), :]


def gelu_pair(v):
    c = math.sqrt(2.0 / math.pi)
    square = v * v
    t = jnp.tanh(c * v * (1.0 + 0.044715 * square))
    half = 0.5 * (1.0 + t)
    slope = half + 0.5 * v * (1.0 - t * t) * (c * (1.0 + 3.0 * 0.044715 * square))
    return v * half, slope


def split_hi_lo(value):
    hi = value.astype(BF16).astype(F32)
    return hi, value - hi


def middle_kernel(*refs):
    slots = refs[:8]
    gain, w_slot, activ_grad = refs[8:11]
    normed, activ, grad_hidden, mean_ref, rstd_ref = refs[11:16]
    payloads = refs[16:24]
    x, first, second = refs[24:]
    low = lanes((HALF, 128)) < 64
    for s in range(8):
        x[:, 128 * s : 128 * s + 128] = slots[s][:PIX, :].astype(F32)
    for t in range(4):
        even = slots[2 * t][PIX:PACK, :].astype(F32)
        odd = slots[2 * t + 1][PIX:PACK, :].astype(F32)
        at = MAIN + 128 * t
        for i in range(ROWS):
            e = even[i * HALF : (i + 1) * HALF]
            o = odd[i * HALF : (i + 1) * HALF]
            x[i * COLS : i * COLS + HALF, at : at + 128] = jnp.where(low, e, swap(o))
            x[i * COLS + HALF : (i + 1) * COLS, at : at + 128] = jnp.where(low, swap(e), o)
    for start in range(0, PIX, GRP):
        rows = slice(start, start + GRP)
        values = x[rows, :]
        mean = jnp.sum(values, axis=1, keepdims=True) * (1.0 / CALL)
        centred = values - mean
        var = jnp.sum(centred * centred, axis=1, keepdims=True) * (1.0 / CALL)
        rstd = 1.0 / jnp.sqrt(var + 1e-06)
        nhat = centred * rstd
        x[rows, :] = nhat
        normed[rows, :] = (nhat * gain[...]).astype(BF16)
        mean_ref[rows, :] = jnp.broadcast_to(mean, (GRP, 128))
        rstd_ref[rows, :] = jnp.broadcast_to(rstd, (GRP, 128))
    for n in range(0, FF, 256):
        hidden = jnp.dot(normed[...], w_slot[:, n : n + 256], preferred_element_type=F32)
        value, slope = gelu_pair(hidden)
        activ[:, n : n + 256] = value.astype(BF16)
        grad_hidden[:, n : n + 256] = (activ_grad[:, n : n + 256] * slope).astype(BF16)
    for t in range(4):
        for at, kind in ((256 * t, 0), (MAIN + 128 * t, 1)):
            width = 128 if kind else 256
            part = lax.dot_general(
                grad_hidden[...],
                w_slot[at : at + width, :],
                (((1,), (1,)), ((), ())),
                preferred_element_type=F32,
            )
            scaled = part * gain[:, at : at + width]
            cross = scaled * x[:, at : at + width]
            if kind == 0:
                scaled = scaled[:, :128] + scaled[:, 128:]
                cross = cross[:, :128] + cross[:, 128:]
                payloads[2 * t][:PIX, :] = part[:, :128].astype(BF16)
                payloads[2 * t + 1][:PIX, :] = part[:, 128:].astype(BF16)
            else:
                evens, odds = [], []
                for i in range(ROWS):
                    l = part[i * COLS : i * COLS + HALF]
                    r = part[i * COLS + HALF : (i + 1) * COLS]
                    evens.append(jnp.where(low, l, swap(r)))
                    odds.append(jnp.where(low, swap(l), r))
                tail = [jnp.zeros((PACK - PIX - REM, 128), F32)]
                payloads[2 * t][PIX:PACK, :] = jnp.concatenate(evens + tail).astype(BF16)
                payloads[2 * t + 1][PIX:PACK, :] = jnp.concatenate(odds + tail).astype(BF16)
            if t == 0 and kind == 0:
                first[...] = scaled
                second[...] = cross
            else:
                first[...] += scaled
                second[...] += cross
    lane = lanes((GRP, 128))
    moments = jnp.zeros((GRP, 128), F32)
    for g in range(PIX // GRP):
        rows = slice(g * GRP, (g + 1) * GRP)
        for q, ref in enumerate((first, second)):
            value = jnp.sum(ref[rows, :], axis=1, keepdims=True) * (1.0 / CALL)
            hi, lo = split_hi_lo(value)
            moments = jnp.where(lane == 32 * q + g, hi, moments)
            moments = jnp.where(lane == 32 * q + 16 + g, lo, moments)
    moments = moments.astype(BF16)
    for s in range(8):
        payloads[s][MOM:PAY, :] = moments


def sum_kernel(a, b, c, d, o_ref):
    total = a[...].astype(F32) + b[...].astype(F32) + c[...].astype(F32) + d[...].astype(F32)
    o_ref[:MOM, :] = total[:MOM].astype(BF16)
    moments = total[MOM:]
    whole = moments + pltpu.roll(moments, 128 - 16, 1)
    hi, lo = split_hi_lo(whole)
    low = (lanes((GRP, 128)) & 31) < 16
    o_ref[MOM:, :] = jnp.where(low, hi, pltpu.roll(lo, 16, 1)).astype(BF16)


def norm_back_kernel(a, b, c, d, e, conv, mean_ref, rstd_ref, gain, o_ref):
    refs = (a, b, c, d, e)
    total = sum(ref[...].astype(F32) for ref in refs[1:]) + a[...].astype(F32)
    moments = total[MOM:]
    whole = moments + pltpu.roll(moments, 128 - 16, 1)
    firsts, seconds = [], []
    for g in range(PIX // GRP):
        firsts.append(jnp.broadcast_to(whole[:, g : g + 1], (GRP, 128)))
        seconds.append(jnp.broadcast_to(whole[:, 32 + g : 33 + g], (GRP, 128)))
    first = jnp.concatenate(firsts)
    second = jnp.concatenate(seconds)
    mean = mean_ref[...]
    rstd = rstd_ref[...]
    main = rstd * (
        total[:PIX] * gain[0:1, :] - first - (conv[:PIX, :].astype(F32) - mean) * rstd * second
    )
    o_ref[:PIX, :] = main.astype(BF16)
    low = lanes((HALF, 128)) < 64

    def folded(v):
        return jnp.concatenate(
            [
                jnp.where(low, v[i * COLS : i * COLS + HALF], v[i * COLS + HALF : (i + 1) * COLS])
                for i in range(ROWS)
            ]
        )

    mean, rstd, first, second = folded(mean), folded(rstd), folded(first), folded(second)
    crem = conv[PIX:PACK, :].astype(F32)[:REM]
    rem = rstd * (total[PIX : PIX + REM] * gain[1:2, :] - first - (crem - mean) * rstd * second)
    rem = jnp.concatenate([rem, jnp.zeros((PACK - PIX - REM, 128), F32)])
    o_ref[PIX:PACK, :] = rem.astype(BF16)


def weights_kernel(scale, blk, place, normed, grad_hidden, activ, mixed, keep, send):
    own = place[0] == 0

    def put(z, w, xlo, rows, zero, one):
        zero, one = zero.astype(BF16), one.astype(BF16)
        keep[z, w, xlo, rows, :] = jnp.where(own, zero, one)
        send[z, w, xlo, rows, :] = jnp.where(own, one, zero)

    def product(left, right):
        return (
            lax.dot_general(left, right, (((0,), (0,)), ((), ())), preferred_element_type=F32)
            * scale
        )

    every = slice(0, 48)
    for t in range(4):
        part = product(mixed[:, 384 * t : 384 * t + 384], activ[...])
        for n in range(2):
            p = part[192 * n : 192 * n + 192]
            put(2 * t + n, 1, 0, every, p[0:48], p[48:96])
            put(2 * t + n, 1, 1, every, p[96:144], p[144:192])
    for t in range(4):
        part = product(normed[:, 256 * t : 256 * t + 256], grad_hidden[...])
        rest = product(normed[:, MAIN + 128 * t : MAIN + 128 * t + 128], grad_hidden[...])
        for n in range(2):
            p = part[128 * n : 128 * n + 128]
            q = rest[64 * n : 64 * n + 64]
            z = blk[2 * t + n]
            put(z, 0, 0, every, p[0:48], p[48:96])
            put(z, 0, 1, every, jnp.concatenate([p[96:128], q[0:16]]), q[16:64])


def call(kernel, outs, args, scratch=(), mib=32, smem=0, flops=0, moved=0):
    space = [pl.BlockSpec(memory_space=pltpu.SMEM)] * smem
    space += [pl.BlockSpec(memory_space=pltpu.VMEM)] * (len(args) - smem)
    single = not isinstance(outs, (list, tuple))
    shapes = [outs] if single else list(outs)
    result = pl.pallas_call(
        kernel,
        out_shape=shapes,
        in_specs=space,
        out_specs=[pl.BlockSpec(memory_space=pltpu.VMEM)] * len(shapes),
        scratch_shapes=list(scratch),
        compiler_params=limit(mib),
        cost_estimate=pl.CostEstimate(flops=flops, bytes_accessed=moved, transcendentals=0),
    )(*args)
    return result[0] if single else result


def shape(dims, dtype):
    return jax.ShapeDtypeStruct(dims, dtype)


def pads():
    return [pltpu.VMEM((9, COLS + 16, 128), F32), pltpu.VMEM((9, HALF + 16, 128), F32)]


def rows_perm(f):
    return [(i, f(i)) for i in range(32)]


def chan_shift(k, x):
    return [(i, ((i // 2 + k) % 4) * 2 + ((i % 2) ^ x)) for i in range(8)]


def halos(block):
    above = lax.ppermute(block, "rows", [(i, i + 1) for i in range(31)])
    below = lax.ppermute(block, "rows", [(i + 1, i) for i in range(31)])
    return above, below


def shards(feature, kernel, ln_gain, layer_scale, w_in, w_out, cotangent):
    scale = 1.0 / math.sqrt(32 * PIX)
    me = lax.axis_index("chan")
    row = lax.axis_index("rows")
    my_y, my_x = me // 2, me % 2
    slots = [(k, x) for k in range(4) for x in range(2)]
    blk = jnp.stack([((my_y + k) % 4) * 2 + (my_x ^ x) for k, x in slots]).astype(jnp.int32)
    place = jnp.stack([row % 2, (row // 2) % 2]).astype(jnp.int32)

    packed = call(pack_kernel, shape((PACK, 128), BF16), [feature])
    above, below = halos(packed)
    taps = kernel.reshape(49, CH)
    taps = jnp.concatenate([taps[:, :128], taps[:, 128:], taps[:, 128:]], axis=1)
    cot = cotangent.reshape(PIX, CALL)
    mixed, activ_grad, w_slot = call(
        first_kernel,
        [shape((PIX, CALL), BF16), shape((PIX, FF), F32), shape((CALL, FF), BF16)],
        [blk, cot, layer_scale.reshape(1, CALL), w_out, w_in],
        smem=1,
        flops=2 * PIX * CALL * FF,
        moved=8 << 20,
    )
    gains = ln_gain.reshape(8, CH)[blk]
    gain_slot = jnp.concatenate([gains[:, :128].reshape(1, -1), gains[:, 128:].reshape(1, -1)], axis=1)
    gain_own = jnp.stack([gains[0, :128], jnp.concatenate([gains[0, 128:], gains[0, 128:]])])
    cot_own = lax.dynamic_slice_in_dim(cotangent, me * CH, CH, 2)

    conv = call(
        conv_kernel, shape((PACK, 128), BF16), [above, packed, below, taps], pads(), flops=1 << 23, moved=1 << 20
    )

    def shift(block, k, x):
        return lax.ppermute(block, "chan", chan_shift(k, x))

    partner = shift(conv, 0, 1)
    gathered = {(0, 0): conv, (0, 1): partner}
    for k in (1, 3, 2):
        gathered[(4 - k) % 4, 0] = shift(conv, k, 0)
    for k in (1, 3, 2):
        gathered[(4 - k) % 4, 1] = shift(partner, k, 0)

    outs = call(
        middle_kernel,
        [
            shape((PIX, CALL), BF16),
            shape((PIX, FF), BF16),
            shape((PIX, FF), BF16),
            shape((PIX, 128), F32),
            shape((PIX, 128), F32),
        ]
        + [shape((PAY, 128), BF16)] * 8,
        [gathered[s] for s in slots] + [gain_slot, w_slot, activ_grad],
        [pltpu.VMEM((PIX, CALL), F32), pltpu.VMEM((PIX, 128), F32), pltpu.VMEM((PIX, 128), F32)],
        mib=40,
        flops=4 * PIX * CALL * FF,
        moved=8 << 20,
    )
    normed, activ, grad_hidden, mean, rstd = outs[:5]
    payload = dict(zip(slots, outs[5:]))

    other = [shift(payload[k, 1], k, 0) for k in (1, 3, 2)]
    mine = [shift(payload[k, 0], k, 0) for k in (1, 3, 2)]
    other_sum = call(sum_kernel, shape((PAY, 128), BF16), [payload[0, 1]] + other, moved=1 << 20)
    crossed = shift(other_sum, 0, 1)

    keep, send = call(
        lambda *refs: weights_kernel(scale, *refs),
        [shape((8, 2, 2, 48, FF), BF16)] * 2,
        [blk, place, normed, grad_hidden, activ, mixed],
        smem=2,
        mib=48,
        flops=4 * PIX * CALL * FF,
        moved=8 << 20,
    )
    got = lax.ppermute(send, "rows", rows_perm(lambda i: i ^ 1))
    both = (keep.astype(F32) + got.astype(F32)).astype(BF16).reshape(8, 192, FF)
    z_groups = [[z * 4 + q for z in range(8)] for q in range(4)]
    z_sum = lax.psum_scatter(
        both, "rows", scatter_dimension=0, axis_index_groups=z_groups, tiled=True
    ).reshape(2, 2, 48, FF)

    grad_conv = call(
        norm_back_kernel,
        shape((PACK, 128), BF16),
        [payload[0, 0]] + mine + [crossed, conv, mean, rstd, gain_own],
        moved=2 << 20,
    )
    grad_above, grad_below = halos(grad_conv)
    terms = call(
        lambda *refs: terms_kernel(scale, *refs),
        shape((112, 128), F32),
        [grad_conv, above, packed, below],
        pads(),
        flops=1 << 23,
        moved=1 << 20,
    )
    for f in (
        lambda i: i ^ 1,
        lambda i: i ^ 2,
        lambda i: i ^ 4,
        lambda i: i ^ 8,
        lambda i: i ^ 16,
    ):
        terms = terms + lax.ppermute(terms, "rows", rows_perm(f))
    grad_kernel = jnp.concatenate([terms[:49], terms[56:105, :64]], axis=1).reshape(7, 7, CH)

    grad_feature = call(
        back_kernel,
        shape((ROWS, COLS, CH), BF16),
        [grad_above, grad_conv, grad_below, taps, cot_own],
        pads(),
        flops=1 << 23,
        moved=1 << 20,
    )

    my_lo = place[1]
    away = lax.dynamic_index_in_dim(z_sum, 1 - my_lo, 1, keepdims=False)
    held = lax.dynamic_index_in_dim(z_sum, my_lo, 1, keepdims=False)
    final = held.astype(F32) + lax.ppermute(away, "rows", rows_perm(lambda i: i ^ 2)).astype(F32)
    return grad_feature, final[0], final[1].T, grad_kernel


def solution(mesh):
    placed = (
        P("rows", None, "chan"),
        P(None, None, "chan"),
        P(),
        P(),
        P(None, "chan"),
        P("chan", None),
        P("rows", None, None),
    )
    return jax.shard_map(
        shards,
        mesh=mesh,
        in_specs=placed,
        out_specs=(
            P("rows", None, "chan"),
            P("rows", "chan"),
            P("chan", "rows"),
            P(None, None, "chan"),
        ),
        check_vma=False,
    )
```

```python
import math

import jax
import jax.numpy as jnp
from jax import lax
from jax.experimental import pallas as pl
from jax.experimental.pallas import tpu as pltpu
from jax.sharding import PartitionSpec as P

F32 = jnp.float32
BF16 = jnp.bfloat16

ROWS = 3
COLS = 144
PIX = ROWS * COLS
HALF = COLS // 2
CH = 192
REM = ROWS * HALF
PACK = 656
MOM = 656
PAY = 704
TERMS = 96
GRP = 48
CALL = 1536
FF = 768
MAIN = 1024


def lanes(shape):
    return lax.broadcasted_iota(jnp.int32, shape, len(shape) - 1)


def swap(x):
    return pltpu.roll(x, 64, x.ndim - 1)


def limit(mib):
    return pltpu.CompilerParams(vmem_limit_bytes=mib * 1024 * 1024)


def my_block():
    return lax.axis_index("chan")


def slot_block(s):
    me = my_block()
    return ((me // 2 + s // 2) % 4) * 2 + (me % 2 + s % 2) % 2


def my_core():
    return lax.axis_index("rows") % 2


def my_lo():
    return (lax.axis_index("rows") // 2) % 2


def pack_kernel(far, o_ref, x_ref, sem):
    copy = pltpu.make_async_copy(far, x_ref, sem.at[0])
    copy.start()
    copy.wait()
    parts = []
    low = lanes((HALF, 128)) < 64
    for i in range(ROWS):
        row = x_ref[i].astype(F32)
        o_ref[i * COLS : (i + 1) * COLS, :] = row[:, :128].astype(BF16)
        rem = jnp.concatenate([row[:, 128:], row[:, 128:]], axis=1)
        parts.append(jnp.where(low, rem[:HALF], rem[HALF:]))
    parts.append(jnp.zeros((PACK - PIX - REM, 128), F32))
    o_ref[PIX:PACK, :] = jnp.concatenate(parts, axis=0).astype(BF16)


def fill_pads(blocks, main_pad, rem_pad):
    low = lanes((8, 128)) < 64
    for n, block in enumerate(blocks):
        main = block[:PIX, :].astype(F32)
        rem = block[PIX:PACK, :].astype(F32)
        for i in range(ROWS):
            r = n * ROWS + i
            main_pad[r, 0:8, :] = jnp.zeros((8, 128), F32)
            main_pad[r, 8 : 8 + COLS, :] = main[i * COLS : (i + 1) * COLS]
            main_pad[r, 8 + COLS : 16 + COLS, :] = jnp.zeros((8, 128), F32)
            part = rem[i * HALF : (i + 1) * HALF]
            rem_pad[r, 8 : 8 + HALF, :] = part
            rem_pad[r, 0:8, :] = jnp.where(low, 0.0, swap(part[HALF - 8 :]))
            rem_pad[r, 8 + HALF : 16 + HALF, :] = jnp.where(low, swap(part[:8]), 0.0)


def taps_block(pad, k_ref, lane0, start, count, flip):
    acc = [None] * ROWS
    for b in range(7):
        for r in range(9):
            window = pad[r, start + 5 + b : start + 5 + b + count, :]
            for i in range(ROWS):
                a = r - i
                if 0 <= a <= 6:
                    tap = (6 - a) * 7 + (6 - b) if flip else a * 7 + b
                    term = window * k_ref[tap : tap + 1, lane0 : lane0 + 128]
                    acc[i] = term if acc[i] is None else acc[i] + term
    return acc


def conv_kernel(top, own, bot, k_ref, o_ref, main_pad, rem_pad):
    fill_pads((top, own, bot), main_pad, rem_pad)
    for start in range(0, COLS, 48):
        acc = taps_block(main_pad, k_ref, 0, start, 48, False)
        for i in range(ROWS):
            o_ref[i * COLS + start : i * COLS + start + 48, :] = acc[i].astype(BF16)
    parts = [[] for _ in range(ROWS)]
    for start in range(0, HALF, 24):
        acc = taps_block(rem_pad, k_ref, 128, start, 24, False)
        for i in range(ROWS):
            parts[i].append(acc[i])
    flat = [p for row in parts for p in row] + [jnp.zeros((PACK - PIX - REM, 128), F32)]
    o_ref[PIX:PACK, :] = jnp.concatenate(flat, axis=0).astype(BF16)


def back_kernel(top, own, bot, k_ref, cot_ref, o_ref, main_pad, rem_pad):
    fill_pads((top, own, bot), main_pad, rem_pad)
    for start in range(0, COLS, 48):
        acc = taps_block(main_pad, k_ref, 0, start, 48, True)
        for i in range(ROWS):
            cot = cot_ref[i * COLS + start : i * COLS + start + 48, :128].astype(F32)
            o_ref[i, start : start + 48, :128] = (acc[i] + cot).astype(BF16)
    parts = [[] for _ in range(ROWS)]
    for start in range(0, HALF, 24):
        acc = taps_block(rem_pad, k_ref, 128, start, 24, True)
        for i in range(ROWS):
            parts[i].append(acc[i])
    for i in range(ROWS):
        rem = jnp.concatenate(parts[i], axis=0)
        both = jnp.concatenate([rem[:, :64], swap(rem)[:, :64]], axis=0)
        cot = cot_ref[i * COLS : (i + 1) * COLS, 128:192].astype(F32)
        o_ref[i, :, 128:] = (both + cot).astype(BF16)


def kernel_terms(grad, top, own, bot, o_ref, main_pad, rem_pad):
    fill_pads((top, own, bot), main_pad, rem_pad)
    o_ref[...] = jnp.zeros((TERMS, 128), F32)
    gmain = grad[:PIX, :].astype(F32)
    grem = grad[PIX:PACK, :].astype(F32)
    for pad, part, width, folded in ((main_pad, gmain, COLS, False), (rem_pad, grem, HALF, True)):
        for b in range(7):
            acc = [jnp.zeros((8, 128), F32)] * 7
            for start in range(0, width, 8):
                windows = [pad[r, start + 5 + b : start + 13 + b, :] for r in range(9)]
                for i in range(ROWS):
                    g = part[i * width + start : i * width + start + 8]
                    for a in range(7):
                        acc[a] = acc[a] + g * windows[i + a]
            for a in range(7):
                total = jnp.sum(acc[a], axis=0, keepdims=True)
                t = a * 7 + b
                if not folded:
                    o_ref[t : t + 1, :] = total
                else:
                    total = total + swap(total)
                    if t < 25:
                        o_ref[64 + t : 65 + t, :64] = total[:, :64]
                    else:
                        o_ref[39 + t : 40 + t, 64:] = total[:, 64:]


def first_kernel(far_cot, far_scale, far_gain, far_taps, w_out, w_in, mixed, activ_grad, w_slot, gain_slot,
                 gain_own, taps_out, cot_own, cot, scale, gain, taps, w_here, sems):
    near = [
        pltpu.make_async_copy(src, dst, sems.at[n])
        for n, (src, dst) in enumerate(
            ((far_scale, scale), (far_cot, cot), (far_gain, gain), (far_taps, taps), (w_out, w_here))
        )
    ]
    late = []
    for s in range(8):
        row = pl.multiple_of(slot_block(s) * CH, 64)
        late.append(
            pltpu.make_async_copy(
                w_in.at[pl.ds(row, 128), :], w_slot.at[pl.ds(128 * s, 128), :], sems.at[5 + 2 * s]
            )
        )
        row = pl.multiple_of(slot_block(s) * CH + 128, 64)
        late.append(
            pltpu.make_async_copy(
                w_in.at[pl.ds(row, 64), :],
                w_slot.at[pl.ds(MAIN + 64 * s, 64), :],
                sems.at[6 + 2 * s],
            )
        )
    for copy in near + late:
        copy.start()
    near[0].wait()
    near[1].wait()
    for j in range(12):
        at = slice(128 * j, 128 * j + 128)
        mixed[:, at] = (cot[:, at].astype(F32) * scale[j : j + 1, :]).astype(BF16)
    near[2].wait()
    near[3].wait()
    for a in range(7):
        rows = slice(7 * a, 7 * a + 7)
        taps_out[rows, :128] = taps[a, :, :128]
        taps_out[rows, 128:192] = taps[a, :, 128:]
        taps_out[rows, 192:] = taps[a, :, 128:]

    def unit(index, high):
        line = gain[pl.ds(index // 2, 1), :]
        return jnp.where(index % 2 == high, line, swap(line))

    low = lanes((1, 128)) < 64
    rest = []
    for s in range(8):
        u = 3 * slot_block(s)
        main = jnp.where(low, unit(u, 0), unit(u + 1, 1))
        gain_slot[:, 128 * s : 128 * s + 128] = main
        rest.append(unit(u + 2, s % 2))
        if s == 0:
            gain_own[0:1, :] = main
            gain_own[1:2, :] = jnp.where(low, rest[0], swap(rest[0]))
    for t in range(4):
        at = MAIN + 128 * t
        gain_slot[:, at : at + 128] = jnp.where(low, rest[2 * t], rest[2 * t + 1])

    def column(index, high):
        at = pl.multiple_of((index // 2) * 128, 128)
        tile = cot[:, pl.ds(at, 128)].astype(F32)
        return jnp.where(index % 2 == high, tile, swap(tile))

    u = 3 * my_block()
    low = lanes((PIX, 128)) < 64
    cot_own[:, :128] = jnp.where(low, column(u, 0), column(u + 1, 1)).astype(BF16)
    cot_own[:, 128:] = column(u + 2, 0).astype(BF16)
    near[4].wait()
    activ_grad[...] = lax.dot_general(
        mixed[...], w_here[...], (((1,), (1,)), ((), ())), preferred_element_type=F32
    )
    for copy in late:
        copy.wait()


def gelu_pair(v):
    c = math.sqrt(2.0 / math.pi)
    square = v * v
    t = jnp.tanh(c * v * (1.0 + 0.044715 * square))
    half = 0.5 * (1.0 + t)
    slope = half + 0.5 * v * (1.0 - t * t) * (c * (1.0 + 3.0 * 0.044715 * square))
    return v * half, slope


def split_hi_lo(value):
    hi = value.astype(BF16).astype(F32)
    return hi, value - hi


def middle_kernel(*refs):
    slots = refs[:8]
    gain, w_slot, activ_grad = refs[8:11]
    normed, activ, grad_hidden, stats = refs[11:15]
    payloads = refs[15:23]
    x, first, second = refs[23:]
    low = lanes((HALF, 128)) < 64
    for s in range(8):
        x[:, 128 * s : 128 * s + 128] = slots[s][:PIX, :].astype(F32)
    for t in range(4):
        even = slots[2 * t][PIX:PACK, :].astype(F32)
        odd = slots[2 * t + 1][PIX:PACK, :].astype(F32)
        at = MAIN + 128 * t
        for i in range(ROWS):
            e = even[i * HALF : (i + 1) * HALF]
            o = odd[i * HALF : (i + 1) * HALF]
            x[i * COLS : i * COLS + HALF, at : at + 128] = jnp.where(low, e, swap(o))
            x[i * COLS + HALF : (i + 1) * COLS, at : at + 128] = jnp.where(low, swap(e), o)
    low = lanes((GRP, 128)) < 64
    for start in range(0, PIX, GRP):
        rows = slice(start, start + GRP)
        values = x[rows, :]
        mean = jnp.sum(values, axis=1, keepdims=True) * (1.0 / CALL)
        centred = values - mean
        var = jnp.sum(centred * centred, axis=1, keepdims=True) * (1.0 / CALL)
        rstd = 1.0 / jnp.sqrt(var + 1e-06)
        nhat = centred * rstd
        x[rows, :] = nhat
        normed[rows, :] = (nhat * gain[...]).astype(BF16)
        stats[rows, :] = jnp.where(
            low, jnp.broadcast_to(mean, (GRP, 128)), jnp.broadcast_to(rstd, (GRP, 128))
        )
    for n in range(0, FF, 256):
        hidden = jnp.dot(normed[...], w_slot[:, n : n + 256], preferred_element_type=F32)
        value, slope = gelu_pair(hidden)
        activ[:, n : n + 256] = value.astype(BF16)
        grad_hidden[:, n : n + 256] = (activ_grad[:, n : n + 256] * slope).astype(BF16)
    low = lanes((HALF, 128)) < 64
    for t in range(4):
        for at, kind in ((256 * t, 0), (MAIN + 128 * t, 1)):
            width = 128 if kind else 256
            part = lax.dot_general(
                grad_hidden[...],
                w_slot[at : at + width, :],
                (((1,), (1,)), ((), ())),
                preferred_element_type=F32,
            )
            scaled = part * gain[:, at : at + width]
            cross = scaled * x[:, at : at + width]
            if kind == 0:
                scaled = scaled[:, :128] + scaled[:, 128:]
                cross = cross[:, :128] + cross[:, 128:]
                payloads[2 * t][:PIX, :] = part[:, :128].astype(BF16)
                payloads[2 * t + 1][:PIX, :] = part[:, 128:].astype(BF16)
            else:
                evens, odds = [], []
                for i in range(ROWS):
                    l = part[i * COLS : i * COLS + HALF]
                    r = part[i * COLS + HALF : (i + 1) * COLS]
                    evens.append(jnp.where(low, l, swap(r)))
                    odds.append(jnp.where(low, swap(l), r))
                tail = [jnp.zeros((PACK - PIX - REM, 128), F32)]
                payloads[2 * t][PIX:PACK, :] = jnp.concatenate(evens + tail).astype(BF16)
                payloads[2 * t + 1][PIX:PACK, :] = jnp.concatenate(odds + tail).astype(BF16)
            if t == 0 and kind == 0:
                first[...] = scaled
                second[...] = cross
            else:
                first[...] += scaled
                second[...] += cross
    lane = lanes((GRP, 128))
    moments = jnp.zeros((GRP, 128), F32)
    for g in range(PIX // GRP):
        rows = slice(g * GRP, (g + 1) * GRP)
        for q, ref in enumerate((first, second)):
            value = jnp.sum(ref[rows, :], axis=1, keepdims=True) * (1.0 / CALL)
            hi, lo = split_hi_lo(value)
            moments = jnp.where(lane == 32 * q + g, hi, moments)
            moments = jnp.where(lane == 32 * q + 16 + g, lo, moments)
    moments = moments.astype(BF16)
    for s in range(8):
        payloads[s][MOM:PAY, :] = moments


def sum_kernel(*refs):
    o_ref = refs[-1]
    total = refs[0][...].astype(F32)
    for ref in refs[1:-1]:
        total = total + ref[...].astype(F32)
    o_ref[:MOM, :] = total[:MOM].astype(BF16)
    moments = total[MOM:]
    whole = moments + pltpu.roll(moments, 128 - 16, 1)
    hi, lo = split_hi_lo(whole)
    low = (lanes((GRP, 128)) & 31) < 16
    o_ref[MOM:, :] = jnp.where(low, hi, pltpu.roll(lo, 16, 1)).astype(BF16)


def norm_back_kernel(a, b, c, d, e, conv, stats, gain, top, own, bot, o_ref, terms, main_pad, rem_pad):
    refs = (a, b, c, d, e)
    total = sum(ref[...].astype(F32) for ref in refs[1:]) + a[...].astype(F32)
    moments = total[MOM:]
    whole = moments + pltpu.roll(moments, 128 - 16, 1)
    firsts, seconds = [], []
    for g in range(PIX // GRP):
        firsts.append(jnp.broadcast_to(whole[:, g : g + 1], (GRP, 128)))
        seconds.append(jnp.broadcast_to(whole[:, 32 + g : 33 + g], (GRP, 128)))
    first = jnp.concatenate(firsts)
    second = jnp.concatenate(seconds)
    both = stats[...]
    low = lanes((PIX, 128)) < 64
    other = swap(both)
    mean = jnp.where(low, both, other)
    rstd = jnp.where(low, other, both)
    main = rstd * (
        total[:PIX] * gain[0:1, :] - first - (conv[:PIX, :].astype(F32) - mean) * rstd * second
    )
    o_ref[:PIX, :] = main.astype(BF16)
    low = lanes((HALF, 128)) < 64

    def folded(v):
        return jnp.concatenate(
            [
                jnp.where(low, v[i * COLS : i * COLS + HALF], v[i * COLS + HALF : (i + 1) * COLS])
                for i in range(ROWS)
            ]
        )

    mean, rstd, first, second = folded(mean), folded(rstd), folded(first), folded(second)
    crem = conv[PIX:PACK, :].astype(F32)[:REM]
    rem = rstd * (total[PIX : PIX + REM] * gain[1:2, :] - first - (crem - mean) * rstd * second)
    rem = jnp.concatenate([rem, jnp.zeros((PACK - PIX - REM, 128), F32)])
    o_ref[PIX:PACK, :] = rem.astype(BF16)
    kernel_terms(o_ref, top, own, bot, terms, main_pad, rem_pad)


def put(own, keep, send, z, xlo, zero, one):
    zero, one = zero.astype(BF16), one.astype(BF16)
    keep[z, xlo, :, :] = jnp.where(own, zero, one)
    send[z, xlo, :, :] = jnp.where(own, one, zero)


def product(left, right):
    return lax.dot_general(left, right, (((0,), (0,)), ((), ())), preferred_element_type=F32)


def weights_out_kernel(activ, mixed, keep, send):
    own = my_core() == 0
    for t in range(4):
        part = product(mixed[:, 384 * t : 384 * t + 384], activ[...])
        for n in range(2):
            p = part[192 * n : 192 * n + 192]
            put(own, keep, send, 2 * t + n, 0, p[0:48], p[48:96])
            put(own, keep, send, 2 * t + n, 1, p[96:144], p[144:192])


def weights_in_kernel(normed, grad_hidden, keep, send):
    own = my_core() == 0
    for t in range(4):
        part = product(normed[:, 256 * t : 256 * t + 256], grad_hidden[...])
        rest = product(normed[:, MAIN + 128 * t : MAIN + 128 * t + 128], grad_hidden[...])
        for n in range(2):
            p = part[128 * n : 128 * n + 128]
            q = rest[64 * n : 64 * n + 64]
            z = slot_block(2 * t + n)
            put(own, keep, send, z, 0, p[0:48], p[48:96])
            put(own, keep, send, z, 1, jnp.concatenate([p[96:128], q[0:16]]), q[16:64])


def join_kernel(keep_in, got_in, keep_out, got_out, far, here, sems):
    copies = []
    for z in range(8):
        for w, (keep, got) in enumerate(((keep_in, got_in), (keep_out, got_out))):
            here[z, w] = (keep[z].astype(F32) + got[z].astype(F32)).astype(BF16)
        copies.append(pltpu.make_async_copy(here.at[z], far.at[z], sems.at[z]))
        copies[-1].start()
    for copy in copies:
        copy.wait()


def pass_kernel(terms, got, *refs):
    refs[len(refs) // 2][...] = terms[...] + got[...]
    for n in range(len(refs) // 2):
        refs[len(refs) // 2 + 1 + n][...] = refs[n][...]


def away_kernel(far, terms, other, o_ref, held, sems):
    copies = []
    for w in range(2):
        rows = pl.ds(48 * w, 48)
        copies.append(pltpu.make_async_copy(far.at[w, 1 - my_lo()], o_ref.at[rows], sems.at[w]))
        copies.append(pltpu.make_async_copy(far.at[w, my_lo()], held.at[rows], sems.at[2 + w]))
    for copy in copies:
        copy.start()
    total = (terms[...] + other[...]).astype(BF16)
    for j in range(6):
        o_ref[96:112, 128 * j : 128 * j + 128] = total[16 * j : 16 * j + 16]
    for copy in copies:
        copy.wait()


def last_kernel(scale, held, away, got, grad_in, grad_out, grad_kernel):
    for w, ref in enumerate((grad_in, grad_out)):
        rows = slice(48 * w, 48 * w + 48)
        ref[...] = (held[rows, :].astype(F32) + got[rows, :].astype(F32)) * scale
    both = (away[96:112, :].astype(F32) + got[96:112, :].astype(F32)) * scale
    lines = jnp.concatenate([both[:, 128 * j : 128 * j + 128] for j in range(6)], axis=0)
    rest = jnp.concatenate([lines[64:89], swap(lines[64:96])[:24]], axis=0)
    for a in range(7):
        grad_kernel[a, :, :128] = lines[7 * a : 7 * a + 7]
        grad_kernel[a, :, 128:] = rest[7 * a : 7 * a + 7, :64]


def call(kernel, outs, args, scratch=(), mib=16, far=(), far_out=False, flops=0, moved=0):
    near = pl.BlockSpec(memory_space=pltpu.VMEM)
    args = [pltpu.with_memory_space_constraint(a, pltpu.HBM) if n in far else a for n, a in enumerate(args)]
    hbm = pl.BlockSpec(memory_space=pltpu.HBM)
    single = not isinstance(outs, (list, tuple))
    shapes = [outs] if single else list(outs)
    result = pl.pallas_call(
        kernel,
        out_shape=shapes,
        in_specs=[hbm if n in far else near for n in range(len(args))],
        out_specs=[hbm if far_out else near] * len(shapes),
        scratch_shapes=list(scratch),
        compiler_params=limit(mib),
        cost_estimate=pl.CostEstimate(flops=flops, bytes_accessed=moved, transcendentals=0),
    )(*args)
    return result[0] if single else result


def shape(dims, dtype):
    return jax.ShapeDtypeStruct(dims, dtype)


def pads():
    return [pltpu.VMEM((9, COLS + 16, 128), F32), pltpu.VMEM((9, HALF + 16, 128), F32)]


def rows_perm(f):
    return [(i, f(i)) for i in range(32)]


def chan_shift(k, x):
    return [(i, ((i // 2 + k) % 4) * 2 + ((i % 2) ^ x)) for i in range(8)]


def halos(block):
    above = lax.ppermute(block, "rows", [(i, i + 1) for i in range(31)])
    below = lax.ppermute(block, "rows", [(i + 1, i) for i in range(31)])
    return above, below


def shards(feature, kernel, ln_gain, layer_scale, w_in, w_out, cotangent):
    scale = 1.0 / math.sqrt(32 * PIX)
    slots = [(k, x) for k in range(4) for x in range(2)]

    packed = call(
        pack_kernel,
        shape((PACK, 128), BF16),
        [feature],
        [pltpu.VMEM((ROWS, COLS, CH), BF16), pltpu.SemaphoreType.DMA((1,))],
        far=(0,),
    )
    above, below = halos(packed)
    mixed, activ_grad, w_slot, gain_slot, gain_own, taps, cot_own = call(
        first_kernel,
        [
            shape((PIX, CALL), BF16),
            shape((PIX, FF), F32),
            shape((CALL, FF), BF16),
            shape((1, CALL), F32),
            shape((2, 128), F32),
            shape((49, 256), F32),
            shape((PIX, 256), BF16),
        ],
        [
            cotangent.reshape(PIX, CALL),
            layer_scale.reshape(12, 128),
            ln_gain.reshape(12, 128),
            kernel,
            w_out,
            w_in,
        ],
        [
            pltpu.VMEM((PIX, CALL), BF16),
            pltpu.VMEM((12, 128), F32),
            pltpu.VMEM((12, 128), F32),
            pltpu.VMEM((7, 7, CH), F32),
            pltpu.VMEM((FF, CALL), BF16),
            pltpu.SemaphoreType.DMA((21,)),
        ],
        far=range(6),
        flops=2 * PIX * CALL * FF,
        moved=8 << 20,
    )

    conv = call(
        conv_kernel, shape((PACK, 128), BF16), [above, packed, below, taps], pads(), flops=1 << 23, moved=1 << 20
    )

    def shift(block, k, x):
        return lax.ppermute(block, "chan", chan_shift(k, x))

    partner = shift(conv, 0, 1)
    gathered = {(0, 0): conv, (0, 1): partner}
    for k in (2, 1, 3):
        gathered[(4 - k) % 4, 0] = shift(conv, k, 0)
    for k in (1, 3):
        gathered[(4 - k) % 4, 1] = shift(partner, k, 0)
    gathered[2, 1] = shift(gathered[2, 0], 0, 1)

    outs = call(
        middle_kernel,
        [
            shape((PIX, CALL), BF16),
            shape((PIX, FF), BF16),
            shape((PIX, FF), BF16),
            shape((PIX, 128), F32),
        ]
        + [shape((PAY, 128), BF16)] * 8,
        [gathered[s] for s in slots] + [gain_slot, w_slot, activ_grad],
        [pltpu.VMEM((PIX, CALL), F32), pltpu.VMEM((PIX, 128), F32), pltpu.VMEM((PIX, 128), F32)],
        mib=16,
        flops=4 * PIX * CALL * FF,
        moved=8 << 20,
    )
    normed, activ, grad_hidden, stats = outs[:4]
    payload = dict(zip(slots, outs[4:]))

    across = shift(payload[2, 1], 0, 1)
    other = [shift(payload[k, 1], k, 0) for k in (1, 3)]
    far_sum = call(sum_kernel, shape((PAY, 128), BF16), [payload[2, 0], across], moved=1 << 20)
    mine = [shift(far_sum, 2, 0)] + [shift(payload[k, 0], k, 0) for k in (1, 3)]
    other_sum = call(sum_kernel, shape((PAY, 128), BF16), [payload[0, 1]] + other, moved=1 << 20)
    crossed = shift(other_sum, 0, 1)

    pairs = [shape((8, 2, 48, FF), BF16)] * 2
    core = rows_perm(lambda i: i ^ 1)
    keep_out, send_out = call(
        weights_out_kernel, pairs, [activ, mixed], flops=2 * PIX * CALL * FF, moved=8 << 20
    )
    got_out = lax.ppermute(send_out, "rows", core)
    keep_in, send_in = call(
        weights_in_kernel,
        pairs,
        [normed, grad_hidden],
        flops=2 * PIX * CALL * FF,
        moved=8 << 20,
    )
    got_in = lax.ppermute(send_in, "rows", core)
    joined = call(
        join_kernel,
        shape((8, 2, 2, 48, FF), BF16),
        [keep_in, got_in, keep_out, got_out],
        [pltpu.VMEM((8, 2, 2, 48, FF), BF16), pltpu.SemaphoreType.DMA((8,))],
        far_out=True,
        moved=8 << 20,
    ).reshape(8, 192, FF)
    z_groups = [[z * 4 + q for z in range(8)] for q in range(4)]
    z_sum = lax.psum_scatter(
        joined, "rows", scatter_dimension=0, axis_index_groups=z_groups, tiled=True
    ).reshape(2, 2, 48, FF)

    grad_conv, terms = call(
        norm_back_kernel,
        [shape((PACK, 128), BF16), shape((TERMS, 128), F32)],
        [payload[0, 0]] + mine + [crossed, conv, stats, gain_own, above, packed, below],
        pads(),
        flops=1 << 23,
        moved=2 << 20,
    )

    def partner_terms(terms, f):
        return lax.ppermute(terms, "rows", rows_perm(f))

    def step(terms, f, *rest):
        return call(
            pass_kernel,
            [shape((TERMS, 128), F32)] + [shape((PACK, 128), BF16)] * len(rest),
            [terms, partner_terms(terms, f)] + list(rest),
            moved=1 << 20,
        )

    terms, grad_conv = step(terms, lambda i: i ^ 1, grad_conv)
    grad_above, grad_below = halos(grad_conv)
    terms, grad_above, grad_below = step(terms, lambda i: i ^ 4, grad_above, grad_below)
    terms = terms + partner_terms(terms, lambda i: i ^ 8)
    grad_feature = call(
        back_kernel,
        shape((ROWS, COLS, CH), BF16),
        [grad_above, grad_conv, grad_below, taps, cot_own],
        pads(),
        flops=1 << 23,
        moved=1 << 20,
    )
    away, held = call(
        away_kernel,
        [shape((112, FF), BF16), shape((96, FF), BF16)],
        [z_sum, terms, partner_terms(terms, lambda i: i ^ 16)],
        [pltpu.SemaphoreType.DMA((4,))],
        far=(0,),
        moved=1 << 20,
    )
    got = lax.ppermute(away, "rows", rows_perm(lambda i: i ^ 2))
    grad_in, grad_out, grad_kernel = call(
        lambda *refs: last_kernel(scale, *refs),
        [shape((48, FF), F32), shape((48, FF), F32), shape((7, 7, CH), F32)],
        [held, away, got],
        moved=1 << 20,
    )
    return grad_feature, grad_in, grad_out.T, grad_kernel


def solution(mesh):
    placed = (
        P("rows", None, "chan"),
        P(None, None, "chan"),
        P(),
        P(),
        P(None, "chan"),
        P("chan", None),
        P("rows", None, None),
    )
    return jax.shard_map(
        shards,
        mesh=mesh,
        in_specs=placed,
        out_specs=(
            P("rows", None, "chan"),
            P("rows", "chan"),
            P("chan", "rows"),
            P(None, None, "chan"),
        ),
        check_vma=False,
    )
```

```python
import math

import jax
import jax.numpy as jnp
from jax import lax
from jax.experimental import pallas as pl
from jax.experimental.pallas import tpu as pltpu
from jax.sharding import PartitionSpec as P

F32 = jnp.float32
BF16 = jnp.bfloat16

ROWS = 3
COLS = 144
PIX = ROWS * COLS
HALF = COLS // 2
CH = 192
REM = ROWS * HALF
PACK = 656
MOM = 656
PAY = 704
TERMS = 96
WEIGHTY = 1 << 35
GRP = 48
CALL = 1536
FF = 768
MAIN = 1024


def lanes(shape):
    return lax.broadcasted_iota(jnp.int32, shape, len(shape) - 1)


def swap(x):
    return pltpu.roll(x, 64, x.ndim - 1)


def limit(mib):
    return pltpu.CompilerParams(vmem_limit_bytes=mib * 1024 * 1024)


def my_block():
    return lax.axis_index("chan")


def slot_block(s):
    me = my_block()
    return ((me // 2 + s // 2) % 4) * 2 + (me % 2 + s % 2) % 2


def my_core():
    return lax.axis_index("rows") % 2


def other_neighbour():
    pairs = [(i, i + 1) for i in range(1, 31, 2)]
    return pairs + [(b, a) for a, b in pairs]


def my_lo():
    return (lax.axis_index("rows") // 2) % 2


def pack_kernel(far, o_ref, x_ref, sem):
    copy = pltpu.make_async_copy(far, x_ref, sem.at[0])
    copy.start()
    copy.wait()
    parts = []
    low = lanes((HALF, 128)) < 64
    for i in range(ROWS):
        row = x_ref[i].astype(F32)
        o_ref[i * COLS : (i + 1) * COLS, :] = row[:, :128].astype(BF16)
        rem = jnp.concatenate([row[:, 128:], row[:, 128:]], axis=1)
        parts.append(jnp.where(low, rem[:HALF], rem[HALF:]))
    parts.append(jnp.zeros((PACK - PIX - REM, 128), F32))
    o_ref[PIX:PACK, :] = jnp.concatenate(parts, axis=0).astype(BF16)


def fill_pads(blocks, main_pad, rem_pad):
    low = lanes((8, 128)) < 64
    odd = my_core() == 1
    core, own, other = blocks

    def either(a, b, rows):
        return jnp.where(odd, a[rows, :].astype(F32), b[rows, :].astype(F32))

    whole, tail = slice(0, PIX), slice(PIX, PACK)
    parts = (
        (either(core, other, whole), either(core, other, tail)),
        (own[whole, :].astype(F32), own[tail, :].astype(F32)),
        (either(other, core, whole), either(other, core, tail)),
    )
    for n, (main, rem) in enumerate(parts):
        for i in range(ROWS):
            r = n * ROWS + i
            main_pad[r, 0:8, :] = jnp.zeros((8, 128), F32)
            main_pad[r, 8 : 8 + COLS, :] = main[i * COLS : (i + 1) * COLS]
            main_pad[r, 8 + COLS : 16 + COLS, :] = jnp.zeros((8, 128), F32)
            part = rem[i * HALF : (i + 1) * HALF]
            rem_pad[r, 8 : 8 + HALF, :] = part
            rem_pad[r, 0:8, :] = jnp.where(low, 0.0, swap(part[HALF - 8 :]))
            rem_pad[r, 8 + HALF : 16 + HALF, :] = jnp.where(low, swap(part[:8]), 0.0)


def taps_block(pad, k_ref, lane0, start, count, flip):
    acc = [None] * ROWS
    for b in range(7):
        for r in range(9):
            window = pad[r, start + 5 + b : start + 5 + b + count, :]
            for i in range(ROWS):
                a = r - i
                if 0 <= a <= 6:
                    tap = (6 - a) * 7 + (6 - b) if flip else a * 7 + b
                    term = window * k_ref[tap : tap + 1, lane0 : lane0 + 128]
                    acc[i] = term if acc[i] is None else acc[i] + term
    return acc


def conv_kernel(top, own, bot, k_ref, o_ref, main_pad, rem_pad):
    fill_pads((top, own, bot), main_pad, rem_pad)
    for start in range(0, COLS, 48):
        acc = taps_block(main_pad, k_ref, 0, start, 48, False)
        for i in range(ROWS):
            o_ref[i * COLS + start : i * COLS + start + 48, :] = acc[i].astype(BF16)
    parts = [[] for _ in range(ROWS)]
    for start in range(0, HALF, 24):
        acc = taps_block(rem_pad, k_ref, 128, start, 24, False)
        for i in range(ROWS):
            parts[i].append(acc[i])
    flat = [p for row in parts for p in row] + [jnp.zeros((PACK - PIX - REM, 128), F32)]
    o_ref[PIX:PACK, :] = jnp.concatenate(flat, axis=0).astype(BF16)


def back_kernel(top, own, bot, k_ref, cot_ref, o_ref, main_pad, rem_pad):
    fill_pads((top, own, bot), main_pad, rem_pad)
    for start in range(0, COLS, 48):
        acc = taps_block(main_pad, k_ref, 0, start, 48, True)
        for i in range(ROWS):
            cot = cot_ref[i * COLS + start : i * COLS + start + 48, :128].astype(F32)
            o_ref[i, start : start + 48, :128] = (acc[i] + cot).astype(BF16)
    parts = [[] for _ in range(ROWS)]
    for start in range(0, HALF, 24):
        acc = taps_block(rem_pad, k_ref, 128, start, 24, True)
        for i in range(ROWS):
            parts[i].append(acc[i])
    for i in range(ROWS):
        rem = jnp.concatenate(parts[i], axis=0)
        both = jnp.concatenate([rem[:, :64], swap(rem)[:, :64]], axis=0)
        cot = cot_ref[i * COLS : (i + 1) * COLS, 128:192].astype(F32)
        o_ref[i, :, 128:] = (both + cot).astype(BF16)


def kernel_terms(grad, top, own, bot, o_ref, main_pad, rem_pad):
    fill_pads((top, own, bot), main_pad, rem_pad)
    o_ref[...] = jnp.zeros((TERMS, 128), F32)
    gmain = grad[:PIX, :].astype(F32)
    grem = grad[PIX:PACK, :].astype(F32)
    for pad, part, width, folded in ((main_pad, gmain, COLS, False), (rem_pad, grem, HALF, True)):
        for b in range(7):
            acc = [jnp.zeros((8, 128), F32)] * 7
            for start in range(0, width, 8):
                windows = [pad[r, start + 5 + b : start + 13 + b, :] for r in range(9)]
                for i in range(ROWS):
                    g = part[i * width + start : i * width + start + 8]
                    for a in range(7):
                        acc[a] = acc[a] + g * windows[i + a]
            for a in range(7):
                total = jnp.sum(acc[a], axis=0, keepdims=True)
                t = a * 7 + b
                if not folded:
                    o_ref[t : t + 1, :] = total
                else:
                    total = total + swap(total)
                    if t < 25:
                        o_ref[64 + t : 65 + t, :64] = total[:, :64]
                    else:
                        o_ref[39 + t : 40 + t, 64:] = total[:, 64:]


def first_kernel(far_cot, far_scale, far_gain, far_taps, w_out, w_in, mixed, activ_grad, w_slot, gain_slot,
                 gain_own, taps_out, cot_own, cot, scale, gain, taps, w_here, sems):
    near = [
        pltpu.make_async_copy(src, dst, sems.at[n])
        for n, (src, dst) in enumerate(
            ((far_scale, scale), (far_cot, cot), (far_gain, gain), (far_taps, taps), (w_out, w_here))
        )
    ]
    late = []
    for s in range(8):
        row = pl.multiple_of(slot_block(s) * CH, 64)
        late.append(
            pltpu.make_async_copy(
                w_in.at[pl.ds(row, 128), :], w_slot.at[pl.ds(128 * s, 128), :], sems.at[5 + 2 * s]
            )
        )
        row = pl.multiple_of(slot_block(s) * CH + 128, 64)
        late.append(
            pltpu.make_async_copy(
                w_in.at[pl.ds(row, 64), :],
                w_slot.at[pl.ds(MAIN + 64 * s, 64), :],
                sems.at[6 + 2 * s],
            )
        )
    for copy in near + late:
        copy.start()
    near[0].wait()
    near[1].wait()
    for j in range(12):
        at = slice(128 * j, 128 * j + 128)
        mixed[:, at] = (cot[:, at].astype(F32) * scale[j : j + 1, :]).astype(BF16)
    near[2].wait()
    near[3].wait()
    for a in range(7):
        rows = slice(7 * a, 7 * a + 7)
        taps_out[rows, :128] = taps[a, :, :128]
        taps_out[rows, 128:192] = taps[a, :, 128:]
        taps_out[rows, 192:] = taps[a, :, 128:]

    def unit(index, high):
        line = gain[pl.ds(index // 2, 1), :]
        return jnp.where(index % 2 == high, line, swap(line))

    low = lanes((1, 128)) < 64
    rest = []
    for s in range(8):
        u = 3 * slot_block(s)
        main = jnp.where(low, unit(u, 0), unit(u + 1, 1))
        gain_slot[:, 128 * s : 128 * s + 128] = main
        rest.append(unit(u + 2, s % 2))
        if s == 0:
            gain_own[0:1, :] = main
            gain_own[1:2, :] = jnp.where(low, rest[0], swap(rest[0]))
    for t in range(4):
        at = MAIN + 128 * t
        gain_slot[:, at : at + 128] = jnp.where(low, rest[2 * t], rest[2 * t + 1])

    def column(index, high):
        at = pl.multiple_of((index // 2) * 128, 128)
        tile = cot[:, pl.ds(at, 128)].astype(F32)
        return jnp.where(index % 2 == high, tile, swap(tile))

    u = 3 * my_block()
    low = lanes((PIX, 128)) < 64
    cot_own[:, :128] = jnp.where(low, column(u, 0), column(u + 1, 1)).astype(BF16)
    cot_own[:, 128:] = column(u + 2, 0).astype(BF16)
    near[4].wait()
    activ_grad[...] = lax.dot_general(
        mixed[...], w_here[...], (((1,), (1,)), ((), ())), preferred_element_type=F32
    )
    for copy in late:
        copy.wait()


def gelu_pair(v):
    c = math.sqrt(2.0 / math.pi)
    square = v * v
    t = jnp.tanh(c * v * (1.0 + 0.044715 * square))
    half = 0.5 * (1.0 + t)
    slope = half + 0.5 * v * (1.0 - t * t) * (c * (1.0 + 3.0 * 0.044715 * square))
    return v * half, slope


def split_hi_lo(value):
    hi = value.astype(BF16).astype(F32)
    return hi, value - hi


def middle_kernel(*refs):
    slots = refs[:8]
    gain, w_slot, activ_grad = refs[8:11]
    normed, activ, grad_hidden, stats = refs[11:15]
    payloads = refs[15:23]
    x, first, second = refs[23:]
    low = lanes((HALF, 128)) < 64
    for s in range(8):
        x[:, 128 * s : 128 * s + 128] = slots[s][:PIX, :].astype(F32)
    for t in range(4):
        even = slots[2 * t][PIX:PACK, :].astype(F32)
        odd = slots[2 * t + 1][PIX:PACK, :].astype(F32)
        at = MAIN + 128 * t
        for i in range(ROWS):
            e = even[i * HALF : (i + 1) * HALF]
            o = odd[i * HALF : (i + 1) * HALF]
            x[i * COLS : i * COLS + HALF, at : at + 128] = jnp.where(low, e, swap(o))
            x[i * COLS + HALF : (i + 1) * COLS, at : at + 128] = jnp.where(low, swap(e), o)
    low = lanes((GRP, 128)) < 64
    for start in range(0, PIX, GRP):
        rows = slice(start, start + GRP)
        values = x[rows, :]
        mean = jnp.sum(values, axis=1, keepdims=True) * (1.0 / CALL)
        centred = values - mean
        var = jnp.sum(centred * centred, axis=1, keepdims=True) * (1.0 / CALL)
        rstd = 1.0 / jnp.sqrt(var + 1e-06)
        nhat = centred * rstd
        x[rows, :] = nhat
        normed[rows, :] = (nhat * gain[...]).astype(BF16)
        stats[rows, :] = jnp.where(
            low, jnp.broadcast_to(mean, (GRP, 128)), jnp.broadcast_to(rstd, (GRP, 128))
        )
    for n in range(0, FF, 256):
        hidden = jnp.dot(normed[...], w_slot[:, n : n + 256], preferred_element_type=F32)
        value, slope = gelu_pair(hidden)
        activ[:, n : n + 256] = value.astype(BF16)
        grad_hidden[:, n : n + 256] = (activ_grad[:, n : n + 256] * slope).astype(BF16)
    low = lanes((HALF, 128)) < 64
    for t in range(4):
        for at, kind in ((256 * t, 0), (MAIN + 128 * t, 1)):
            width = 128 if kind else 256
            part = lax.dot_general(
                grad_hidden[...],
                w_slot[at : at + width, :],
                (((1,), (1,)), ((), ())),
                preferred_element_type=F32,
            )
            scaled = part * gain[:, at : at + width]
            cross = scaled * x[:, at : at + width]
            if kind == 0:
                scaled = scaled[:, :128] + scaled[:, 128:]
                cross = cross[:, :128] + cross[:, 128:]
                payloads[2 * t][:PIX, :] = part[:, :128].astype(BF16)
                payloads[2 * t + 1][:PIX, :] = part[:, 128:].astype(BF16)
            else:
                evens, odds = [], []
                for i in range(ROWS):
                    l = part[i * COLS : i * COLS + HALF]
                    r = part[i * COLS + HALF : (i + 1) * COLS]
                    evens.append(jnp.where(low, l, swap(r)))
                    odds.append(jnp.where(low, swap(l), r))
                tail = [jnp.zeros((PACK - PIX - REM, 128), F32)]
                payloads[2 * t][PIX:PACK, :] = jnp.concatenate(evens + tail).astype(BF16)
                payloads[2 * t + 1][PIX:PACK, :] = jnp.concatenate(odds + tail).astype(BF16)
            if t == 0 and kind == 0:
                first[...] = scaled
                second[...] = cross
            else:
                first[...] += scaled
                second[...] += cross
    lane = lanes((GRP, 128))
    moments = jnp.zeros((GRP, 128), F32)
    for g in range(PIX // GRP):
        rows = slice(g * GRP, (g + 1) * GRP)
        for q, ref in enumerate((first, second)):
            value = jnp.sum(ref[rows, :], axis=1, keepdims=True) * (1.0 / CALL)
            hi, lo = split_hi_lo(value)
            moments = jnp.where(lane == 32 * q + g, hi, moments)
            moments = jnp.where(lane == 32 * q + 16 + g, lo, moments)
    moments = moments.astype(BF16)
    for s in range(8):
        payloads[s][MOM:PAY, :] = moments


def sum_payloads(refs, o_ref):
    total = refs[0][...].astype(F32)
    for ref in refs[1:]:
        total = total + ref[...].astype(F32)
    o_ref[:MOM, :] = total[:MOM].astype(BF16)
    moments = total[MOM:]
    whole = moments + pltpu.roll(moments, 128 - 16, 1)
    hi, lo = split_hi_lo(whole)
    low = (lanes((GRP, 128)) & 31) < 16
    o_ref[MOM:, :] = jnp.where(low, hi, pltpu.roll(lo, 16, 1)).astype(BF16)


def middle_sums_kernel(far, across, other, one, three, own_one, own_three, *outs):
    sum_payloads((other, one, three), outs[0])
    sum_payloads((far, across), outs[1])
    outs[2][...] = own_one[...]
    outs[3][...] = own_three[...]


def norm_back_kernel(a, b, c, d, e, conv, stats, gain, top, own, bot, o_ref, both_ref, terms, main_pad, rem_pad):
    refs = (a, b, c, d, e)
    total = sum(ref[...].astype(F32) for ref in refs[1:]) + a[...].astype(F32)
    moments = total[MOM:]
    whole = moments + pltpu.roll(moments, 128 - 16, 1)
    firsts, seconds = [], []
    for g in range(PIX // GRP):
        firsts.append(jnp.broadcast_to(whole[:, g : g + 1], (GRP, 128)))
        seconds.append(jnp.broadcast_to(whole[:, 32 + g : 33 + g], (GRP, 128)))
    first = jnp.concatenate(firsts)
    second = jnp.concatenate(seconds)
    both = stats[...]
    low = lanes((PIX, 128)) < 64
    other = swap(both)
    mean = jnp.where(low, both, other)
    rstd = jnp.where(low, other, both)
    main = rstd * (
        total[:PIX] * gain[0:1, :] - first - (conv[:PIX, :].astype(F32) - mean) * rstd * second
    )
    o_ref[:PIX, :] = main.astype(BF16)
    low = lanes((HALF, 128)) < 64

    def folded(v):
        return jnp.concatenate(
            [
                jnp.where(low, v[i * COLS : i * COLS + HALF], v[i * COLS + HALF : (i + 1) * COLS])
                for i in range(ROWS)
            ]
        )

    mean, rstd, first, second = folded(mean), folded(rstd), folded(first), folded(second)
    crem = conv[PIX:PACK, :].astype(F32)[:REM]
    rem = rstd * (total[PIX : PIX + REM] * gain[1:2, :] - first - (crem - mean) * rstd * second)
    rem = jnp.concatenate([rem, jnp.zeros((PACK - PIX - REM, 128), F32)])
    o_ref[PIX:PACK, :] = rem.astype(BF16)
    kernel_terms(o_ref, top, own, bot, terms, main_pad, rem_pad)
    both_ref[:PACK, :] = o_ref[...]
    both_ref[PACK:, :] = terms[...].astype(BF16)


def put(own, keep, send, z, xlo, zero, one):
    zero, one = zero.astype(BF16), one.astype(BF16)
    keep[z, xlo, :, :] = jnp.where(own, zero, one)
    send[z, xlo, :, :] = jnp.where(own, one, zero)


def product(left, right):
    return lax.dot_general(left, right, (((0,), (0,)), ((), ())), preferred_element_type=F32)


def weights_out_kernel(activ, mixed, keep, send):
    own = my_core() == 0
    for t in range(4):
        part = product(mixed[:, 384 * t : 384 * t + 384], activ[...])
        for n in range(2):
            p = part[192 * n : 192 * n + 192]
            put(own, keep, send, 2 * t + n, 0, p[0:48], p[48:96])
            put(own, keep, send, 2 * t + n, 1, p[96:144], p[144:192])


def weights_in_kernel(normed, grad_hidden, keep, send):
    own = my_core() == 0
    for t in range(4):
        part = product(normed[:, 256 * t : 256 * t + 256], grad_hidden[...])
        rest = product(normed[:, MAIN + 128 * t : MAIN + 128 * t + 128], grad_hidden[...])
        for n in range(2):
            p = part[128 * n : 128 * n + 128]
            q = rest[64 * n : 64 * n + 64]
            z = slot_block(2 * t + n)
            put(own, keep, send, z, 0, p[0:48], p[48:96])
            put(own, keep, send, z, 1, jnp.concatenate([p[96:128], q[0:16]]), q[16:64])


HALVES = ((0, 3, 4, 7), (1, 2, 5, 6))
PAIRS = (((0, 1), (2, 3)), ((0, 3), (1, 2)))


def kind_of(z):
    return 0 if z in HALVES[0] else 1


def pair_of(z):
    kind = kind_of(z)
    return next(q for q in range(2) if HALVES[kind].index(z) in PAIRS[kind][q])


def second_partner(z):
    return (z + (1 if z % 2 else -1)) % 8


def third_partner(z):
    half = HALVES[kind_of(z)]
    pair = [half[place] for place in PAIRS[kind_of(z)][pair_of(z)]]
    return pair[1 - pair.index(z)]


def by_z(table):
    z = lax.axis_index("rows") // 4
    value = 0
    for n, entry in enumerate(table):
        value = jnp.where(z == n, entry, value)
    return value


def added(a, b):
    return (a.astype(F32) + b.astype(F32)).astype(BF16)


def half_blocks(n):
    mine = by_z([HALVES[kind_of(z)][n] for z in range(8)])
    theirs = by_z([HALVES[1 - kind_of(z)][n] for z in range(8)])
    return mine, theirs


def join_half_kernel(keep, got, keep_next, send_next):
    for n in range(4):
        mine, theirs = half_blocks(n)
        keep_next[n] = added(keep[mine], got[mine])
        send_next[n] = added(keep[theirs], got[theirs])


def join_out_kernel(keep, got, keep_next, send_next):
    lo = my_lo()
    for z in range(8):
        keep_next[z] = added(keep[z, lo], got[z, lo])
        send_next[z] = added(keep[z, 1 - lo], got[z, 1 - lo])


def join_lo_kernel(keep, got, keep_next, send_next):
    lo = my_lo()
    for n in range(4):
        keep_next[n] = added(keep[n, lo], got[n, lo])
        send_next[n] = added(keep[n, 1 - lo], got[n, 1 - lo])


def put_terms(o_ref, at, total):
    for j in range(6):
        o_ref[at : at + 16, 128 * j : 128 * j + 128] = total[16 * j : 16 * j + 16]


def take_terms(ref, at):
    return jnp.concatenate(
        [ref[at : at + 16, 128 * j : 128 * j + 128].astype(F32) for j in range(6)], axis=0
    )


def join_pair_kernel(keep_in, got_in, keep_out, got_out, keep_next, send_next):
    for n in range(2):
        mine = by_z([PAIRS[kind_of(z)][pair_of(z)][n] for z in range(8)])
        theirs = by_z([PAIRS[kind_of(z)][1 - pair_of(z)][n] for z in range(8)])
        for w, (keep, other) in enumerate(((keep_in, got_in), (keep_out, got_out))):
            rows = slice(96 * n + 48 * w, 96 * n + 48 * w + 48)
            keep_next[rows, :] = added(keep[mine], other[mine])
            send_next[rows, :] = added(keep[theirs], other[theirs])


def join_one_kernel(keep, other, terms, got, keep_next, send_next):
    second = by_z([PAIRS[kind_of(z)][pair_of(z)].index(HALVES[kind_of(z)].index(z)) for z in range(8)])
    mine = pl.multiple_of(96 * second, 32)
    theirs = pl.multiple_of(96 - 96 * second, 32)
    keep_next[...] = added(keep[pl.ds(mine, 96), :], other[pl.ds(mine, 96), :])
    send_next[:96, :] = added(keep[pl.ds(theirs, 96), :], other[pl.ds(theirs, 96), :])
    put_terms(send_next, 96, (terms[...] + got[...]).astype(BF16))


def pass_kernel(terms, got, block, o_ref, block_ref):
    o_ref[...] = terms[...] + got[...]
    block_ref[...] = block[...]


def open_kernel(sent, got, o_ref):
    o_ref[...] = sent[PACK:, :].astype(F32) + got[PACK:, :].astype(F32)


def last_kernel(scale, keep, sent, got, grad_in, grad_out, grad_kernel):
    for w, ref in enumerate((grad_in, grad_out)):
        rows = slice(48 * w, 48 * w + 48)
        ref[...] = (keep[rows, :].astype(F32) + got[rows, :].astype(F32)) * scale
    lines = (take_terms(sent, 96) + take_terms(got, 96)) * scale
    rest = jnp.concatenate([lines[64:89], swap(lines[64:96])[:24]], axis=0)
    for a in range(7):
        grad_kernel[a, :, :128] = lines[7 * a : 7 * a + 7]
        grad_kernel[a, :, 128:] = rest[7 * a : 7 * a + 7, :64]


def call(kernel, outs, args, scratch=(), mib=16, far=(), after=(), flops=0, moved=0):
    count = len(args)
    args = list(args) + list(after)

    def body(*refs):
        kernel(*refs[:count], *refs[len(args) :])

    near = pl.BlockSpec(memory_space=pltpu.VMEM)
    args = [pltpu.with_memory_space_constraint(a, pltpu.HBM) if n in far else a for n, a in enumerate(args)]
    hbm = pl.BlockSpec(memory_space=pltpu.HBM)
    single = not isinstance(outs, (list, tuple))
    shapes = [outs] if single else list(outs)
    result = pl.pallas_call(
        body,
        out_shape=shapes,
        in_specs=[hbm if n in far else near for n in range(len(args))],
        out_specs=[near] * len(shapes),
        scratch_shapes=list(scratch),
        compiler_params=limit(mib),
        cost_estimate=pl.CostEstimate(flops=flops, bytes_accessed=moved, transcendentals=0),
    )(*args)
    return result[0] if single else result


def shape(dims, dtype):
    return jax.ShapeDtypeStruct(dims, dtype)


def pads():
    return [pltpu.VMEM((9, COLS + 16, 128), F32), pltpu.VMEM((9, HALF + 16, 128), F32)]


def rows_perm(f):
    return [(i, f(i)) for i in range(32)]


def chan_shift(k, x):
    return [(i, ((i // 2 + k) % 4) * 2 + ((i % 2) ^ x)) for i in range(8)]


def other_side(block):
    return lax.ppermute(block, "rows", other_neighbour())


def shards(feature, kernel, ln_gain, layer_scale, w_in, w_out, cotangent):
    scale = 1.0 / math.sqrt(32 * PIX)
    slots = [(k, x) for k in range(4) for x in range(2)]

    packed = call(
        pack_kernel,
        shape((PACK, 128), BF16),
        [feature],
        [pltpu.VMEM((ROWS, COLS, CH), BF16), pltpu.SemaphoreType.DMA((1,))],
        far=(0,),
    )
    core = rows_perm(lambda i: i ^ 1)
    above, below = lax.ppermute(packed, "rows", core), other_side(packed)
    mixed, activ_grad, w_slot, gain_slot, gain_own, taps, cot_own = call(
        first_kernel,
        [
            shape((PIX, CALL), BF16),
            shape((PIX, FF), F32),
            shape((CALL, FF), BF16),
            shape((1, CALL), F32),
            shape((2, 128), F32),
            shape((49, 256), F32),
            shape((PIX, 256), BF16),
        ],
        [
            cotangent.reshape(PIX, CALL),
            layer_scale.reshape(12, 128),
            ln_gain.reshape(12, 128),
            kernel,
            w_out,
            w_in,
        ],
        [
            pltpu.VMEM((PIX, CALL), BF16),
            pltpu.VMEM((12, 128), F32),
            pltpu.VMEM((12, 128), F32),
            pltpu.VMEM((7, 7, CH), F32),
            pltpu.VMEM((FF, CALL), BF16),
            pltpu.SemaphoreType.DMA((21,)),
        ],
        far=range(6),
        flops=2 * PIX * CALL * FF,
        moved=8 << 20,
    )

    conv = call(
        conv_kernel, shape((PACK, 128), BF16), [above, packed, below, taps], pads(), flops=1 << 23, moved=1 << 20
    )

    def shift(block, k, x):
        return lax.ppermute(block, "chan", chan_shift(k, x))

    partner = shift(conv, 0, 1)
    gathered = {(0, 0): conv, (0, 1): partner}
    for k in (2, 1, 3):
        gathered[(4 - k) % 4, 0] = shift(conv, k, 0)
    for k in (1, 3):
        gathered[(4 - k) % 4, 1] = shift(partner, k, 0)
    gathered[2, 1] = shift(gathered[2, 0], 0, 1)

    outs = call(
        middle_kernel,
        [
            shape((PIX, CALL), BF16),
            shape((PIX, FF), BF16),
            shape((PIX, FF), BF16),
            shape((PIX, 128), F32),
        ]
        + [shape((PAY, 128), BF16)] * 8,
        [gathered[s] for s in slots] + [gain_slot, w_slot, activ_grad],
        [pltpu.VMEM((PIX, CALL), F32), pltpu.VMEM((PIX, 128), F32), pltpu.VMEM((PIX, 128), F32)],
        mib=16,
        flops=4 * PIX * CALL * FF,
        moved=8 << 20,
    )
    normed, activ, grad_hidden, stats = outs[:4]
    payload = dict(zip(slots, outs[4:]))

    across = shift(payload[2, 1], 0, 1)
    other = [shift(payload[k, 1], k, 0) for k in (1, 3)]
    pairs = [shape((8, 2, 48, FF), BF16)] * 2
    keep_out, send_out = call(
        weights_out_kernel, pairs, [activ, mixed], flops=2 * PIX * CALL * FF, moved=8 << 20
    )
    got_out = lax.ppermute(send_out, "rows", core)
    keep_in, send_in = call(
        weights_in_kernel, pairs, [normed, grad_hidden], flops=2 * PIX * CALL * FF, moved=8 << 20
    )
    got_in = lax.ppermute(send_in, "rows", core)
    other_sum, far_sum, own_one, own_three = call(
        middle_sums_kernel,
        [shape((PAY, 128), BF16)] * 4,
        [payload[2, 0], across, payload[0, 1]] + other + [payload[1, 0], payload[3, 0]],
        after=[send_out, send_in],
        moved=1 << 20,
    )
    crossed = shift(other_sum, 0, 1)
    mine = [shift(far_sum, 2, 0), shift(own_one, 1, 0), shift(own_three, 3, 0)]

    def move(block, f):
        return lax.ppermute(block, "rows", rows_perm(f))

    def blocks(*dims):
        return shape(dims + (48, FF), BF16)

    def to_z(f):
        return lambda i: 4 * f(i // 4) + i % 4

    def to_lo(i):
        return i ^ 2

    def exchange(joiner, keep, got, dims, f, moved, after):
        keep, send = call(joiner, [blocks(*dims)] * 2, [keep, got], after=[after], moved=moved)
        return keep, move(send, f)

    def first(z):
        return z ^ 1

    keep_out, got_out = exchange(join_out_kernel, keep_out, got_out, (8,), to_lo, 4 << 20, other_sum)
    keep_in, got_in = exchange(join_half_kernel, keep_in, got_in, (4, 2), to_z(first), 4 << 20, far_sum)
    grad_conv, sent, terms = call(
        norm_back_kernel,
        [shape((PACK, 128), BF16), shape((PACK + TERMS, 128), BF16), shape((TERMS, 128), F32)],
        [payload[0, 0]] + mine + [crossed, conv, stats, gain_own, above, packed, below],
        pads(),
        flops=WEIGHTY,
        moved=2 << 20,
    )

    def partner_terms(terms, f):
        return lax.ppermute(terms, "rows", rows_perm(f))

    grad_side = other_side(grad_conv)
    grad_core = lax.ppermute(sent, "rows", core)
    terms = call(open_kernel, shape((TERMS, 128), F32), [sent, grad_core])
    terms = terms + partner_terms(terms, to_lo)
    keep_out, got_out = exchange(join_half_kernel, keep_out, got_out, (4,), to_z(first), 2 << 20, terms)
    keep_in, got_in = exchange(join_lo_kernel, keep_in, got_in, (4,), to_lo, 2 << 20, terms)
    terms, grad_side = call(
        pass_kernel,
        [shape((TERMS, 128), F32), shape((PACK, 128), BF16)],
        [terms, partner_terms(terms, to_z(first)), grad_side],
        moved=1 << 20,
    )
    keep, send = call(
        join_pair_kernel,
        [shape((192, FF), BF16), shape((192, FF), BF16)],
        [keep_in, got_in, keep_out, got_out],
        after=[terms],
        moved=2 << 20,
    )
    got = move(send, to_z(second_partner))

    grad_feature = call(
        back_kernel,
        shape((ROWS, COLS, CH), BF16),
        [grad_core, grad_conv, grad_side, taps, cot_own],
        pads(),
        flops=1 << 23,
        moved=1 << 20,
    )
    keep, sent = call(
        join_one_kernel,
        [shape((96, FF), BF16), shape((112, FF), BF16)],
        [keep, got, terms, partner_terms(terms, to_z(second_partner))],
        moved=1 << 20,
    )
    got = move(sent, to_z(third_partner))
    grad_in, grad_out, grad_kernel = call(
        lambda *refs: last_kernel(scale, *refs),
        [shape((48, FF), F32), shape((48, FF), F32), shape((7, 7, CH), F32)],
        [keep, sent, got],
        moved=1 << 20,
    )
    return grad_feature, grad_in, grad_out.T, grad_kernel


def solution(mesh):
    placed = (
        P("rows", None, "chan"),
        P(None, None, "chan"),
        P(),
        P(),
        P(None, "chan"),
        P("chan", None),
        P("rows", None, None),
    )
    return jax.shard_map(
        shards,
        mesh=mesh,
        in_specs=placed,
        out_specs=(
            P("rows", None, "chan"),
            P("rows", "chan"),
            P("chan", "rows"),
            P(None, None, "chan"),
        ),
        check_vma=False,
    )
```

```python
import math

import jax
import jax.numpy as jnp
from jax import lax
from jax.experimental import pallas as pl
from jax.experimental.pallas import tpu as pltpu
from jax.sharding import PartitionSpec as P

F32 = jnp.float32
BF16 = jnp.bfloat16

ROWS = 3
COLS = 144
PIX = ROWS * COLS
HALF = COLS // 2
CH = 192
REM = ROWS * HALF
PACK = 656
MOM = 656
PAY = 704
TERMS = 96
COST_BACK = 1 << 35
COST_OUT = 1 << 30
COST_PASS = 1 << 20
COST_FAR = 1 << 20
COST_IN = 1 << 30
COST_SUMS = 1 << 20
GRP = 48
CALL = 1536
FF = 768
MAIN = 1024


def lanes(shape):
    return lax.broadcasted_iota(jnp.int32, shape, len(shape) - 1)


def swap(x):
    return pltpu.roll(x, 64, x.ndim - 1)


def limit(mib):
    return pltpu.CompilerParams(vmem_limit_bytes=mib * 1024 * 1024)


def my_block():
    return lax.axis_index("chan")


def slot_block(s):
    me = my_block()
    return ((me // 2 + s // 2) % 4) * 2 + (me % 2 + s % 2) % 2


def my_core():
    return lax.axis_index("rows") % 2


def other_neighbour():
    pairs = [(i, i + 1) for i in range(1, 31, 2)]
    return pairs + [(b, a) for a, b in pairs]


def my_lo():
    return (lax.axis_index("rows") // 2) % 2


def pack_kernel(far, o_ref, x_ref, sem):
    copy = pltpu.make_async_copy(far, x_ref, sem.at[0])
    copy.start()
    copy.wait()
    parts = []
    low = lanes((HALF, 128)) < 64
    for i in range(ROWS):
        row = x_ref[i].astype(F32)
        o_ref[i * COLS : (i + 1) * COLS, :] = row[:, :128].astype(BF16)
        rem = jnp.concatenate([row[:, 128:], row[:, 128:]], axis=1)
        parts.append(jnp.where(low, rem[:HALF], rem[HALF:]))
    parts.append(jnp.zeros((PACK - PIX - REM, 128), F32))
    o_ref[PIX:PACK, :] = jnp.concatenate(parts, axis=0).astype(BF16)


def fill_pads(blocks, main_pad, rem_pad):
    low = lanes((8, 128)) < 64
    odd = my_core() == 1
    core, own, other = blocks

    def either(a, b, rows):
        return jnp.where(odd, a[rows, :].astype(F32), b[rows, :].astype(F32))

    whole, tail = slice(0, PIX), slice(PIX, PACK)
    parts = (
        (either(core, other, whole), either(core, other, tail)),
        (own[whole, :].astype(F32), own[tail, :].astype(F32)),
        (either(other, core, whole), either(other, core, tail)),
    )
    for n, (main, rem) in enumerate(parts):
        for i in range(ROWS):
            r = n * ROWS + i
            main_pad[r, 0:8, :] = jnp.zeros((8, 128), F32)
            main_pad[r, 8 : 8 + COLS, :] = main[i * COLS : (i + 1) * COLS]
            main_pad[r, 8 + COLS : 16 + COLS, :] = jnp.zeros((8, 128), F32)
            part = rem[i * HALF : (i + 1) * HALF]
            rem_pad[r, 8 : 8 + HALF, :] = part
            rem_pad[r, 0:8, :] = jnp.where(low, 0.0, swap(part[HALF - 8 :]))
            rem_pad[r, 8 + HALF : 16 + HALF, :] = jnp.where(low, swap(part[:8]), 0.0)


def taps_block(pad, k_ref, lane0, start, count, flip):
    acc = [None] * ROWS
    for b in range(7):
        for r in range(9):
            window = pad[r, start + 5 + b : start + 5 + b + count, :]
            for i in range(ROWS):
                a = r - i
                if 0 <= a <= 6:
                    tap = (6 - a) * 7 + (6 - b) if flip else a * 7 + b
                    term = window * k_ref[tap : tap + 1, lane0 : lane0 + 128]
                    acc[i] = term if acc[i] is None else acc[i] + term
    return acc


def conv_kernel(top, own, bot, k_ref, o_ref, main_pad, rem_pad):
    fill_pads((top, own, bot), main_pad, rem_pad)
    for start in range(0, COLS, 48):
        acc = taps_block(main_pad, k_ref, 0, start, 48, False)
        for i in range(ROWS):
            o_ref[i * COLS + start : i * COLS + start + 48, :] = acc[i].astype(BF16)
    parts = [[] for _ in range(ROWS)]
    for start in range(0, HALF, 24):
        acc = taps_block(rem_pad, k_ref, 128, start, 24, False)
        for i in range(ROWS):
            parts[i].append(acc[i])
    flat = [p for row in parts for p in row] + [jnp.zeros((PACK - PIX - REM, 128), F32)]
    o_ref[PIX:PACK, :] = jnp.concatenate(flat, axis=0).astype(BF16)


def back_kernel(top, own, bot, k_ref, cot_ref, o_ref, main_pad, rem_pad):
    fill_pads((top, own, bot), main_pad, rem_pad)
    for start in range(0, COLS, 48):
        acc = taps_block(main_pad, k_ref, 0, start, 48, True)
        for i in range(ROWS):
            cot = cot_ref[i * COLS + start : i * COLS + start + 48, :128].astype(F32)
            o_ref[i, start : start + 48, :128] = (acc[i] + cot).astype(BF16)
    parts = [[] for _ in range(ROWS)]
    for start in range(0, HALF, 24):
        acc = taps_block(rem_pad, k_ref, 128, start, 24, True)
        for i in range(ROWS):
            parts[i].append(acc[i])
    for i in range(ROWS):
        rem = jnp.concatenate(parts[i], axis=0)
        both = jnp.concatenate([rem[:, :64], swap(rem)[:, :64]], axis=0)
        cot = cot_ref[i * COLS : (i + 1) * COLS, 128:192].astype(F32)
        o_ref[i, :, 128:] = (both + cot).astype(BF16)


def kernel_terms(grad, top, own, bot, o_ref, main_pad, rem_pad):
    fill_pads((top, own, bot), main_pad, rem_pad)
    o_ref[...] = jnp.zeros((TERMS, 128), F32)
    gmain = grad[:PIX, :].astype(F32)
    grem = grad[PIX:PACK, :].astype(F32)
    for pad, part, width, folded in ((main_pad, gmain, COLS, False), (rem_pad, grem, HALF, True)):
        for b in range(7):
            acc = [jnp.zeros((8, 128), F32)] * 7
            for start in range(0, width, 8):
                windows = [pad[r, start + 5 + b : start + 13 + b, :] for r in range(9)]
                for i in range(ROWS):
                    g = part[i * width + start : i * width + start + 8]
                    for a in range(7):
                        acc[a] = acc[a] + g * windows[i + a]
            for a in range(7):
                total = jnp.sum(acc[a], axis=0, keepdims=True)
                t = a * 7 + b
                if not folded:
                    o_ref[t : t + 1, :] = total
                else:
                    total = total + swap(total)
                    if t < 25:
                        o_ref[64 + t : 65 + t, :64] = total[:, :64]
                    else:
                        o_ref[39 + t : 40 + t, 64:] = total[:, 64:]


def first_kernel(far_cot, far_scale, far_gain, far_taps, w_out, w_in, mixed, activ_grad, w_slot, gain_slot,
                 gain_own, taps_out, cot_own, cot, scale, gain, taps, w_here, sems):
    near = [
        pltpu.make_async_copy(src, dst, sems.at[n])
        for n, (src, dst) in enumerate(
            ((far_scale, scale), (far_cot, cot), (far_gain, gain), (far_taps, taps), (w_out, w_here))
        )
    ]
    late = []
    for s in range(8):
        row = pl.multiple_of(slot_block(s) * CH, 64)
        late.append(
            pltpu.make_async_copy(
                w_in.at[pl.ds(row, 128), :], w_slot.at[pl.ds(128 * s, 128), :], sems.at[5 + 2 * s]
            )
        )
        row = pl.multiple_of(slot_block(s) * CH + 128, 64)
        late.append(
            pltpu.make_async_copy(
                w_in.at[pl.ds(row, 64), :],
                w_slot.at[pl.ds(MAIN + 64 * s, 64), :],
                sems.at[6 + 2 * s],
            )
        )
    for copy in near + late:
        copy.start()
    near[0].wait()
    near[1].wait()
    for j in range(12):
        at = slice(128 * j, 128 * j + 128)
        mixed[:, at] = (cot[:, at].astype(F32) * scale[j : j + 1, :]).astype(BF16)
    near[2].wait()
    near[3].wait()
    for a in range(7):
        rows = slice(7 * a, 7 * a + 7)
        taps_out[rows, :128] = taps[a, :, :128]
        taps_out[rows, 128:192] = taps[a, :, 128:]
        taps_out[rows, 192:] = taps[a, :, 128:]

    def unit(index, high):
        line = gain[pl.ds(index // 2, 1), :]
        return jnp.where(index % 2 == high, line, swap(line))

    low = lanes((1, 128)) < 64
    rest = []
    for s in range(8):
        u = 3 * slot_block(s)
        main = jnp.where(low, unit(u, 0), unit(u + 1, 1))
        gain_slot[:, 128 * s : 128 * s + 128] = main
        rest.append(unit(u + 2, s % 2))
        if s == 0:
            gain_own[0:1, :] = main
            gain_own[1:2, :] = jnp.where(low, rest[0], swap(rest[0]))
    for t in range(4):
        at = MAIN + 128 * t
        gain_slot[:, at : at + 128] = jnp.where(low, rest[2 * t], rest[2 * t + 1])

    def column(index, high):
        at = pl.multiple_of((index // 2) * 128, 128)
        tile = cot[:, pl.ds(at, 128)].astype(F32)
        return jnp.where(index % 2 == high, tile, swap(tile))

    u = 3 * my_block()
    low = lanes((PIX, 128)) < 64
    cot_own[:, :128] = jnp.where(low, column(u, 0), column(u + 1, 1)).astype(BF16)
    cot_own[:, 128:] = column(u + 2, 0).astype(BF16)
    near[4].wait()
    activ_grad[...] = lax.dot_general(
        mixed[...], w_here[...], (((1,), (1,)), ((), ())), preferred_element_type=F32
    )
    for copy in late:
        copy.wait()


def gelu_pair(v):
    c = math.sqrt(2.0 / math.pi)
    square = v * v
    t = jnp.tanh(c * v * (1.0 + 0.044715 * square))
    half = 0.5 * (1.0 + t)
    slope = half + 0.5 * v * (1.0 - t * t) * (c * (1.0 + 3.0 * 0.044715 * square))
    return v * half, slope


def split_hi_lo(value):
    hi = value.astype(BF16).astype(F32)
    return hi, value - hi


def middle_kernel(*refs):
    slots = refs[:8]
    gain, w_slot, activ_grad = refs[8:11]
    normed, activ, grad_hidden, stats = refs[11:15]
    payloads = list(refs[15:19]) + [refs[19].at[x] for x in range(2)] + [refs[20].at[x] for x in range(2)]
    payloads = [payloads[n] for n in (0, 1, 4, 5, 2, 3, 6, 7)]
    x, first, second = refs[21:]
    low = lanes((HALF, 128)) < 64
    for s in range(8):
        x[:, 128 * s : 128 * s + 128] = slots[s][:PIX, :].astype(F32)
    for t in range(4):
        even = slots[2 * t][PIX:PACK, :].astype(F32)
        odd = slots[2 * t + 1][PIX:PACK, :].astype(F32)
        at = MAIN + 128 * t
        for i in range(ROWS):
            e = even[i * HALF : (i + 1) * HALF]
            o = odd[i * HALF : (i + 1) * HALF]
            x[i * COLS : i * COLS + HALF, at : at + 128] = jnp.where(low, e, swap(o))
            x[i * COLS + HALF : (i + 1) * COLS, at : at + 128] = jnp.where(low, swap(e), o)
    low = lanes((GRP, 128)) < 64
    for start in range(0, PIX, GRP):
        rows = slice(start, start + GRP)
        values = x[rows, :]
        mean = jnp.sum(values, axis=1, keepdims=True) * (1.0 / CALL)
        centred = values - mean
        var = jnp.sum(centred * centred, axis=1, keepdims=True) * (1.0 / CALL)
        rstd = 1.0 / jnp.sqrt(var + 1e-06)
        nhat = centred * rstd
        x[rows, :] = nhat
        normed[rows, :] = (nhat * gain[...]).astype(BF16)
        stats[rows, :] = jnp.where(
            low, jnp.broadcast_to(mean, (GRP, 128)), jnp.broadcast_to(rstd, (GRP, 128))
        )
    for n in range(0, FF, 256):
        hidden = jnp.dot(normed[...], w_slot[:, n : n + 256], preferred_element_type=F32)
        value, slope = gelu_pair(hidden)
        activ[:, n : n + 256] = value.astype(BF16)
        grad_hidden[:, n : n + 256] = (activ_grad[:, n : n + 256] * slope).astype(BF16)
    low = lanes((HALF, 128)) < 64
    for t in range(4):
        for at, kind in ((256 * t, 0), (MAIN + 128 * t, 1)):
            width = 128 if kind else 256
            part = lax.dot_general(
                grad_hidden[...],
                w_slot[at : at + width, :],
                (((1,), (1,)), ((), ())),
                preferred_element_type=F32,
            )
            scaled = part * gain[:, at : at + width]
            cross = scaled * x[:, at : at + width]
            if kind == 0:
                scaled = scaled[:, :128] + scaled[:, 128:]
                cross = cross[:, :128] + cross[:, 128:]
                payloads[2 * t][:PIX, :] = part[:, :128].astype(BF16)
                payloads[2 * t + 1][:PIX, :] = part[:, 128:].astype(BF16)
            else:
                evens, odds = [], []
                for i in range(ROWS):
                    l = part[i * COLS : i * COLS + HALF]
                    r = part[i * COLS + HALF : (i + 1) * COLS]
                    evens.append(jnp.where(low, l, swap(r)))
                    odds.append(jnp.where(low, swap(l), r))
                tail = [jnp.zeros((PACK - PIX - REM, 128), F32)]
                payloads[2 * t][PIX:PACK, :] = jnp.concatenate(evens + tail).astype(BF16)
                payloads[2 * t + 1][PIX:PACK, :] = jnp.concatenate(odds + tail).astype(BF16)
            if t == 0 and kind == 0:
                first[...] = scaled
                second[...] = cross
            else:
                first[...] += scaled
                second[...] += cross
    lane = lanes((GRP, 128))
    moments = jnp.zeros((GRP, 128), F32)
    for g in range(PIX // GRP):
        rows = slice(g * GRP, (g + 1) * GRP)
        for q, ref in enumerate((first, second)):
            value = jnp.sum(ref[rows, :], axis=1, keepdims=True) * (1.0 / CALL)
            hi, lo = split_hi_lo(value)
            moments = jnp.where(lane == 32 * q + g, hi, moments)
            moments = jnp.where(lane == 32 * q + 16 + g, lo, moments)
    moments = moments.astype(BF16)
    for s in range(8):
        payloads[s][MOM:PAY, :] = moments


def sum_payloads(refs, o_ref):
    total = refs[0][...].astype(F32)
    for ref in refs[1:]:
        total = total + ref[...].astype(F32)
    o_ref[:MOM, :] = total[:MOM].astype(BF16)
    moments = total[MOM:]
    whole = moments + pltpu.roll(moments, 128 - 16, 1)
    hi, lo = split_hi_lo(whole)
    low = (lanes((GRP, 128)) & 31) < 16
    o_ref[MOM:, :] = jnp.where(low, hi, pltpu.roll(lo, 16, 1)).astype(BF16)


def far_sum_kernel(far, across, o_ref):
    sum_payloads((far, across), o_ref)


def other_sum_kernel(other, one, three, o_ref):
    sum_payloads((other, one.at[1], three.at[1]), o_ref)


def norm_back_kernel(a, b, c, d, e, conv, stats, gain, top, own, bot, o_ref, both_ref, terms, main_pad, rem_pad):
    total = a[...].astype(F32) + (b[...].astype(F32) + c[0].astype(F32)) + (d[0].astype(F32) + e[...].astype(F32))
    moments = total[MOM:]
    whole = moments + pltpu.roll(moments, 128 - 16, 1)
    firsts, seconds = [], []
    for g in range(PIX // GRP):
        firsts.append(jnp.broadcast_to(whole[:, g : g + 1], (GRP, 128)))
        seconds.append(jnp.broadcast_to(whole[:, 32 + g : 33 + g], (GRP, 128)))
    first = jnp.concatenate(firsts)
    second = jnp.concatenate(seconds)
    both = stats[...]
    low = lanes((PIX, 128)) < 64
    other = swap(both)
    mean = jnp.where(low, both, other)
    rstd = jnp.where(low, other, both)
    main = rstd * (
        total[:PIX] * gain[0:1, :] - first - (conv[:PIX, :].astype(F32) - mean) * rstd * second
    )
    o_ref[:PIX, :] = main.astype(BF16)
    low = lanes((HALF, 128)) < 64

    def folded(v):
        return jnp.concatenate(
            [
                jnp.where(low, v[i * COLS : i * COLS + HALF], v[i * COLS + HALF : (i + 1) * COLS])
                for i in range(ROWS)
            ]
        )

    mean, rstd, first, second = folded(mean), folded(rstd), folded(first), folded(second)
    crem = conv[PIX:PACK, :].astype(F32)[:REM]
    rem = rstd * (total[PIX : PIX + REM] * gain[1:2, :] - first - (crem - mean) * rstd * second)
    rem = jnp.concatenate([rem, jnp.zeros((PACK - PIX - REM, 128), F32)])
    o_ref[PIX:PACK, :] = rem.astype(BF16)
    kernel_terms(o_ref, top, own, bot, terms, main_pad, rem_pad)
    both_ref[:PACK, :] = o_ref[...]
    both_ref[PACK:, :] = terms[...].astype(BF16)


def put(own, keep, send, z, xlo, zero, one):
    zero, one = zero.astype(BF16), one.astype(BF16)
    keep[z, xlo, :, :] = jnp.where(own, zero, one)
    send[z, xlo, :, :] = jnp.where(own, one, zero)


def product(left, right):
    return lax.dot_general(left, right, (((0,), (0,)), ((), ())), preferred_element_type=F32)


def weights_out_kernel(activ, mixed, keep, send):
    own = my_core() == 0
    for t in range(4):
        part = product(mixed[:, 384 * t : 384 * t + 384], activ[...])
        for n in range(2):
            p = part[192 * n : 192 * n + 192]
            put(own, keep, send, 2 * t + n, 0, p[0:48], p[48:96])
            put(own, keep, send, 2 * t + n, 1, p[96:144], p[144:192])


def weights_in_kernel(normed, grad_hidden, keep, send):
    own = my_core() == 0
    for t in range(4):
        part = product(normed[:, 256 * t : 256 * t + 256], grad_hidden[...])
        rest = product(normed[:, MAIN + 128 * t : MAIN + 128 * t + 128], grad_hidden[...])
        for n in range(2):
            p = part[128 * n : 128 * n + 128]
            q = rest[64 * n : 64 * n + 64]
            z = slot_block(2 * t + n)
            put(own, keep, send, z, 0, p[0:48], p[48:96])
            put(own, keep, send, z, 1, jnp.concatenate([p[96:128], q[0:16]]), q[16:64])


HALVES = ((0, 3, 4, 7), (1, 2, 5, 6))
PAIRS = (((0, 1), (2, 3)), ((0, 3), (1, 2)))


def kind_of(z):
    return 0 if z in HALVES[0] else 1


def pair_of(z):
    kind = kind_of(z)
    return next(q for q in range(2) if HALVES[kind].index(z) in PAIRS[kind][q])


def second_partner(z):
    return (z + (1 if z % 2 else -1)) % 8


def third_partner(z):
    half = HALVES[kind_of(z)]
    pair = [half[place] for place in PAIRS[kind_of(z)][pair_of(z)]]
    return pair[1 - pair.index(z)]


def by_z(table):
    z = lax.axis_index("rows") // 4
    value = 0
    for n, entry in enumerate(table):
        value = jnp.where(z == n, entry, value)
    return value


def added(a, b):
    return (a.astype(F32) + b.astype(F32)).astype(BF16)


def half_blocks(n):
    mine = by_z([HALVES[kind_of(z)][n] for z in range(8)])
    theirs = by_z([HALVES[1 - kind_of(z)][n] for z in range(8)])
    return mine, theirs


def join_half_kernel(keep, got, keep_next, send_next):
    for n in range(4):
        mine, theirs = half_blocks(n)
        keep_next[n] = added(keep[mine], got[mine])
        send_next[n] = added(keep[theirs], got[theirs])


def join_out_kernel(keep, got, keep_next, send_next):
    lo = my_lo()
    for z in range(8):
        keep_next[z] = added(keep[z, lo], got[z, lo])
        send_next[z] = added(keep[z, 1 - lo], got[z, 1 - lo])


def pair_blocks(n):
    mine = by_z([PAIRS[kind_of(z)][pair_of(z)][n] for z in range(8)])
    theirs = by_z([PAIRS[kind_of(z)][1 - pair_of(z)][n] for z in range(8)])
    return mine, theirs


def join_pair_kernel(keep, got, keep_next, send_next):
    for n in range(2):
        mine, theirs = pair_blocks(n)
        keep_next[n] = added(keep[mine], got[mine])
        send_next[n] = added(keep[theirs], got[theirs])


def join_lo_kernel(keep, got, keep_next, send_next):
    lo = my_lo()
    for n in range(2):
        keep_next[n] = added(keep[n, lo], got[n, lo])
        send_next[n] = added(keep[n, 1 - lo], got[n, 1 - lo])


def put_terms(o_ref, at, total):
    for j in range(6):
        o_ref[at : at + 16, 128 * j : 128 * j + 128] = total[16 * j : 16 * j + 16]


def take_terms(ref, at):
    return jnp.concatenate(
        [ref[at : at + 16, 128 * j : 128 * j + 128].astype(F32) for j in range(6)], axis=0
    )


def join_one_kernel(keep_in, got_in, keep_out, got_out, terms, got, keep_next, send_next):
    second = by_z([PAIRS[kind_of(z)][pair_of(z)].index(HALVES[kind_of(z)].index(z)) for z in range(8)])
    for w, (keep, other) in enumerate(((keep_in, got_in), (keep_out, got_out))):
        rows = slice(48 * w, 48 * w + 48)
        keep_next[rows, :] = added(keep[second], other[second])
        send_next[rows, :] = added(keep[1 - second], other[1 - second])
    put_terms(send_next, 96, (terms[...] + got[...]).astype(BF16))


def pass_kernel(terms, got, block, o_ref, block_ref):
    o_ref[...] = terms[...] + got[...]
    block_ref[...] = block[...]


def open_kernel(sent, got, o_ref):
    o_ref[...] = sent[PACK:, :].astype(F32) + got[PACK:, :].astype(F32)


def last_kernel(scale, keep, sent, got, grad_in, grad_out, grad_kernel):
    for w, ref in enumerate((grad_in, grad_out)):
        rows = slice(48 * w, 48 * w + 48)
        ref[...] = (keep[rows, :].astype(F32) + got[rows, :].astype(F32)) * scale
    lines = (take_terms(sent, 96) + take_terms(got, 96)) * scale
    rest = jnp.concatenate([lines[64:89], swap(lines[64:96])[:24]], axis=0)
    for a in range(7):
        grad_kernel[a, :, :128] = lines[7 * a : 7 * a + 7]
        grad_kernel[a, :, 128:] = rest[7 * a : 7 * a + 7, :64]


def call(kernel, outs, args, scratch=(), mib=16, far=(), after=(), flops=0, moved=0):
    count = len(args)
    args = list(args) + list(after)

    def body(*refs):
        kernel(*refs[:count], *refs[len(args) :])

    near = pl.BlockSpec(memory_space=pltpu.VMEM)
    args = [pltpu.with_memory_space_constraint(a, pltpu.HBM) if n in far else a for n, a in enumerate(args)]
    hbm = pl.BlockSpec(memory_space=pltpu.HBM)
    single = not isinstance(outs, (list, tuple))
    shapes = [outs] if single else list(outs)
    result = pl.pallas_call(
        body,
        out_shape=shapes,
        in_specs=[hbm if n in far else near for n in range(len(args))],
        out_specs=[near] * len(shapes),
        scratch_shapes=list(scratch),
        compiler_params=limit(mib),
        cost_estimate=pl.CostEstimate(flops=flops, bytes_accessed=moved, transcendentals=0),
    )(*args)
    return result[0] if single else result


def shape(dims, dtype):
    return jax.ShapeDtypeStruct(dims, dtype)


def pads():
    return [pltpu.VMEM((9, COLS + 16, 128), F32), pltpu.VMEM((9, HALF + 16, 128), F32)]


def rows_perm(f):
    return [(i, f(i)) for i in range(32)]


def chan_shift(k, x):
    return [(i, ((i // 2 + k) % 4) * 2 + ((i % 2) ^ x)) for i in range(8)]


def other_side(block):
    return lax.ppermute(block, "rows", other_neighbour())


def shards(feature, kernel, ln_gain, layer_scale, w_in, w_out, cotangent):
    scale = 1.0 / math.sqrt(32 * PIX)
    slots = [(k, x) for k in range(4) for x in range(2)]

    packed = call(
        pack_kernel,
        shape((PACK, 128), BF16),
        [feature],
        [pltpu.VMEM((ROWS, COLS, CH), BF16), pltpu.SemaphoreType.DMA((1,))],
        far=(0,),
    )
    core = rows_perm(lambda i: i ^ 1)
    above, below = lax.ppermute(packed, "rows", core), other_side(packed)
    mixed, activ_grad, w_slot, gain_slot, gain_own, taps, cot_own = call(
        first_kernel,
        [
            shape((PIX, CALL), BF16),
            shape((PIX, FF), F32),
            shape((CALL, FF), BF16),
            shape((1, CALL), F32),
            shape((2, 128), F32),
            shape((49, 256), F32),
            shape((PIX, 256), BF16),
        ],
        [
            cotangent.reshape(PIX, CALL),
            layer_scale.reshape(12, 128),
            ln_gain.reshape(12, 128),
            kernel,
            w_out,
            w_in,
        ],
        [
            pltpu.VMEM((PIX, CALL), BF16),
            pltpu.VMEM((12, 128), F32),
            pltpu.VMEM((12, 128), F32),
            pltpu.VMEM((7, 7, CH), F32),
            pltpu.VMEM((FF, CALL), BF16),
            pltpu.SemaphoreType.DMA((21,)),
        ],
        far=range(6),
        flops=2 * PIX * CALL * FF,
        moved=8 << 20,
    )

    conv = call(
        conv_kernel, shape((PACK, 128), BF16), [above, packed, below, taps], pads(), flops=1 << 23, moved=1 << 20
    )

    def shift(block, k, x):
        return lax.ppermute(block, "chan", chan_shift(k, x))

    partner = shift(conv, 0, 1)
    gathered = {(0, 0): conv, (0, 1): partner}
    for k in (2, 1, 3):
        gathered[(4 - k) % 4, 0] = shift(conv, k, 0)
    for k in (1, 3):
        gathered[(4 - k) % 4, 1] = shift(partner, k, 0)
    gathered[2, 1] = shift(gathered[2, 0], 0, 1)

    outs = call(
        middle_kernel,
        [
            shape((PIX, CALL), BF16),
            shape((PIX, FF), BF16),
            shape((PIX, FF), BF16),
            shape((PIX, 128), F32),
        ]
        + [shape((PAY, 128), BF16)] * 4
        + [shape((2, PAY, 128), BF16)] * 2,
        [gathered[s] for s in slots] + [gain_slot, w_slot, activ_grad],
        [pltpu.VMEM((PIX, CALL), F32), pltpu.VMEM((PIX, 128), F32), pltpu.VMEM((PIX, 128), F32)],
        mib=16,
        flops=4 * PIX * CALL * FF,
        moved=8 << 20,
    )
    normed, activ, grad_hidden, stats = outs[:4]
    payload = dict(zip(((0, 0), (0, 1), (2, 0), (2, 1), 1, 3), outs[4:]))

    across = shift(payload[2, 1], 0, 1)
    far_sum = call(
        far_sum_kernel, shape((PAY, 128), BF16), [payload[2, 0], across], flops=COST_FAR, moved=1 << 20
    )
    beside = [shift(payload[k], k, 0) for k in (1, 3)]
    other_sum = call(
        other_sum_kernel,
        shape((PAY, 128), BF16),
        [payload[0, 1]] + beside,
        flops=COST_SUMS,
        moved=1 << 20,
    )
    crossed = shift(other_sum, 0, 1)
    mine = [shift(far_sum, 2, 0)] + beside

    pairs = [shape((8, 2, 48, FF), BF16)] * 2
    keep_out, send_out = call(
        weights_out_kernel, pairs, [activ, mixed], flops=COST_OUT, moved=8 << 20
    )
    got_out = lax.ppermute(send_out, "rows", core)
    keep_in, send_in = call(
        weights_in_kernel, pairs, [normed, grad_hidden], after=[other_sum, far_sum], flops=COST_IN, moved=8 << 20
    )
    got_in = lax.ppermute(send_in, "rows", core)
    def move(block, f):
        return lax.ppermute(block, "rows", rows_perm(f))

    def blocks(*dims):
        return shape(dims + (48, FF), BF16)

    def to_z(f):
        return lambda i: 4 * f(i // 4) + i % 4

    def to_lo(i):
        return i ^ 2

    def exchange(joiner, keep, got, dims, f, moved, after=()):
        keep, send = call(joiner, [blocks(*dims)] * 2, [keep, got], after=after, moved=moved)
        return keep, move(send, f)

    def first(z):
        return z ^ 1

    keep_out, got_out = exchange(join_out_kernel, keep_out, got_out, (8,), to_lo, 4 << 20, [other_sum])
    keep_in, got_in = exchange(join_half_kernel, keep_in, got_in, (4, 2), to_z(first), 4 << 20, [other_sum])
    grad_conv, sent, terms = call(
        norm_back_kernel,
        [shape((PACK, 128), BF16), shape((PACK + TERMS, 128), BF16), shape((TERMS, 128), F32)],
        [payload[0, 0]] + mine + [crossed, conv, stats, gain_own, above, packed, below],
        pads(),
        flops=COST_BACK,
        moved=2 << 20,
    )

    def partner_terms(terms, f):
        return lax.ppermute(terms, "rows", rows_perm(f))

    grad_side = other_side(grad_conv)
    grad_core = lax.ppermute(sent, "rows", core)
    terms = call(open_kernel, shape((TERMS, 128), F32), [sent, grad_core])
    terms = terms + partner_terms(terms, to_lo)
    keep_out, got_out = exchange(
        join_half_kernel, keep_out, got_out, (4,), to_z(first), 2 << 20, [terms]
    )
    keep_in, got_in = exchange(
        join_pair_kernel, keep_in, got_in, (2, 2), to_z(second_partner), 2 << 20, [terms]
    )
    terms, grad_side = call(
        pass_kernel,
        [shape((TERMS, 128), F32), shape((PACK, 128), BF16)],
        [terms, partner_terms(terms, to_z(first)), grad_side],
        flops=COST_PASS,
        moved=1 << 20,
    )
    keep_out, got_out = exchange(
        join_pair_kernel, keep_out, got_out, (2,), to_z(second_partner), 1 << 20, [terms]
    )
    keep_in, got_in = exchange(join_lo_kernel, keep_in, got_in, (2,), to_lo, 1 << 20, [terms])

    grad_feature = call(
        back_kernel,
        shape((ROWS, COLS, CH), BF16),
        [grad_core, grad_conv, grad_side, taps, cot_own],
        pads(),
        flops=1 << 23,
        moved=1 << 20,
    )
    keep, sent = call(
        join_one_kernel,
        [shape((96, FF), BF16), shape((112, FF), BF16)],
        [keep_in, got_in, keep_out, got_out, terms, partner_terms(terms, to_z(second_partner))],
        moved=1 << 20,
    )
    got = move(sent, to_z(third_partner))
    grad_in, grad_out, grad_kernel = call(
        lambda *refs: last_kernel(scale, *refs),
        [shape((48, FF), F32), shape((48, FF), F32), shape((7, 7, CH), F32)],
        [keep, sent, got],
        moved=1 << 20,
    )
    return grad_feature, grad_in, grad_out.T, grad_kernel


def solution(mesh):
    placed = (
        P("rows", None, "chan"),
        P(None, None, "chan"),
        P(),
        P(),
        P(None, "chan"),
        P("chan", None),
        P("rows", None, None),
    )
    return jax.shard_map(
        shards,
        mesh=mesh,
        in_specs=placed,
        out_specs=(
            P("rows", None, "chan"),
            P("rows", "chan"),
            P("chan", "rows"),
            P(None, None, "chan"),
        ),
        check_vma=False,
    )
```

```python
import math

import jax
import jax.numpy as jnp
from jax import lax
from jax.experimental import pallas as pl
from jax.experimental.pallas import tpu as pltpu
from jax.sharding import PartitionSpec as P

F32 = jnp.float32
BF16 = jnp.bfloat16

ROWS = 3
COLS = 144
PIX = ROWS * COLS
HALF = COLS // 2
CH = 192
REM = ROWS * HALF
PACK = 656
MOM = 656
PAY = 704
TERMS = 96
COST_BACK = 1 << 35
COST_OUT = 1 << 30
COST_PASS = 1 << 20
COST_FAR = 1 << 20
COST_IN = 1 << 30
COST_SUMS = 1 << 20
GRP = 48
CALL = 1536
FF = 768
MAIN = 1024


def lanes(shape):
    return lax.broadcasted_iota(jnp.int32, shape, len(shape) - 1)


def swap(x):
    return pltpu.roll(x, 64, x.ndim - 1)


def limit(mib):
    return pltpu.CompilerParams(vmem_limit_bytes=mib * 1024 * 1024)


def my_block():
    return lax.axis_index("chan")


def slot_block(s):
    me = my_block()
    return ((me // 2 + s // 2) % 4) * 2 + (me % 2 + s % 2) % 2


def my_core():
    return lax.axis_index("rows") % 2


def other_neighbour():
    pairs = [(i, i + 1) for i in range(1, 31, 2)]
    return pairs + [(b, a) for a, b in pairs]


def my_lo():
    return (lax.axis_index("rows") // 2) % 2


def pack_kernel(far, o_ref, x_ref, sem):
    copy = pltpu.make_async_copy(far, x_ref, sem.at[0])
    copy.start()
    copy.wait()
    parts = []
    low = lanes((HALF, 128)) < 64
    for i in range(ROWS):
        row = x_ref[i].astype(F32)
        o_ref[i * COLS : (i + 1) * COLS, :] = row[:, :128].astype(BF16)
        rem = jnp.concatenate([row[:, 128:], row[:, 128:]], axis=1)
        parts.append(jnp.where(low, rem[:HALF], rem[HALF:]))
    parts.append(jnp.zeros((PACK - PIX - REM, 128), F32))
    o_ref[PIX:PACK, :] = jnp.concatenate(parts, axis=0).astype(BF16)


def fill_pads(blocks, main_pad, rem_pad):
    low = lanes((8, 128)) < 64
    odd = my_core() == 1
    core, own, other = blocks

    def either(a, b, rows):
        return jnp.where(odd, a[rows, :].astype(F32), b[rows, :].astype(F32))

    whole, tail = slice(0, PIX), slice(PIX, PACK)
    parts = (
        (either(core, other, whole), either(core, other, tail)),
        (own[whole, :].astype(F32), own[tail, :].astype(F32)),
        (either(other, core, whole), either(other, core, tail)),
    )
    for n, (main, rem) in enumerate(parts):
        for i in range(ROWS):
            r = n * ROWS + i
            main_pad[r, 0:8, :] = jnp.zeros((8, 128), F32)
            main_pad[r, 8 : 8 + COLS, :] = main[i * COLS : (i + 1) * COLS]
            main_pad[r, 8 + COLS : 16 + COLS, :] = jnp.zeros((8, 128), F32)
            part = rem[i * HALF : (i + 1) * HALF]
            rem_pad[r, 8 : 8 + HALF, :] = part
            rem_pad[r, 0:8, :] = jnp.where(low, 0.0, swap(part[HALF - 8 :]))
            rem_pad[r, 8 + HALF : 16 + HALF, :] = jnp.where(low, swap(part[:8]), 0.0)


def taps_block(pad, k_ref, lane0, start, count, flip):
    acc = [None] * ROWS
    for b in range(7):
        for r in range(9):
            window = pad[r, start + 5 + b : start + 5 + b + count, :]
            for i in range(ROWS):
                a = r - i
                if 0 <= a <= 6:
                    tap = (6 - a) * 7 + (6 - b) if flip else a * 7 + b
                    term = window * k_ref[tap : tap + 1, lane0 : lane0 + 128]
                    acc[i] = term if acc[i] is None else acc[i] + term
    return acc


def conv_kernel(top, own, bot, k_ref, o_ref, main_pad, rem_pad):
    fill_pads((top, own, bot), main_pad, rem_pad)
    for start in range(0, COLS, 48):
        acc = taps_block(main_pad, k_ref, 0, start, 48, False)
        for i in range(ROWS):
            o_ref[i * COLS + start : i * COLS + start + 48, :] = acc[i].astype(BF16)
    parts = [[] for _ in range(ROWS)]
    for start in range(0, HALF, 24):
        acc = taps_block(rem_pad, k_ref, 128, start, 24, False)
        for i in range(ROWS):
            parts[i].append(acc[i])
    flat = [p for row in parts for p in row] + [jnp.zeros((PACK - PIX - REM, 128), F32)]
    o_ref[PIX:PACK, :] = jnp.concatenate(flat, axis=0).astype(BF16)


def back_kernel(top, own, bot, k_ref, cot_ref, o_ref, main_pad, rem_pad):
    fill_pads((top, own, bot), main_pad, rem_pad)
    for start in range(0, COLS, 48):
        acc = taps_block(main_pad, k_ref, 0, start, 48, True)
        for i in range(ROWS):
            cot = cot_ref[i * COLS + start : i * COLS + start + 48, :128].astype(F32)
            o_ref[i, start : start + 48, :128] = (acc[i] + cot).astype(BF16)
    parts = [[] for _ in range(ROWS)]
    for start in range(0, HALF, 24):
        acc = taps_block(rem_pad, k_ref, 128, start, 24, True)
        for i in range(ROWS):
            parts[i].append(acc[i])
    for i in range(ROWS):
        rem = jnp.concatenate(parts[i], axis=0)
        both = jnp.concatenate([rem[:, :64], swap(rem)[:, :64]], axis=0)
        cot = cot_ref[i * COLS : (i + 1) * COLS, 128:192].astype(F32)
        o_ref[i, :, 128:] = (both + cot).astype(BF16)


def kernel_terms(grad, top, own, bot, o_ref, main_pad, rem_pad):
    fill_pads((top, own, bot), main_pad, rem_pad)
    o_ref[...] = jnp.zeros((TERMS, 128), F32)
    gmain = grad[:PIX, :].astype(F32)
    grem = grad[PIX:PACK, :].astype(F32)
    for pad, part, width, folded in ((main_pad, gmain, COLS, False), (rem_pad, grem, HALF, True)):
        for b in range(7):
            acc = [jnp.zeros((8, 128), F32)] * 7
            for start in range(0, width, 8):
                windows = [pad[r, start + 5 + b : start + 13 + b, :] for r in range(9)]
                for i in range(ROWS):
                    g = part[i * width + start : i * width + start + 8]
                    for a in range(7):
                        acc[a] = acc[a] + g * windows[i + a]
            for a in range(7):
                total = jnp.sum(acc[a], axis=0, keepdims=True)
                t = a * 7 + b
                if not folded:
                    o_ref[t : t + 1, :] = total
                else:
                    total = total + swap(total)
                    if t < 25:
                        o_ref[64 + t : 65 + t, :64] = total[:, :64]
                    else:
                        o_ref[39 + t : 40 + t, 64:] = total[:, 64:]


def first_kernel(far_cot, far_scale, far_gain, far_taps, w_out, w_in, mixed, activ_grad, w_slot, gain_slot,
                 gain_own, taps_out, cot_own, cot, scale, gain, taps, w_here, sems):
    near = [
        pltpu.make_async_copy(src, dst, sems.at[n])
        for n, (src, dst) in enumerate(
            ((far_scale, scale), (far_cot, cot), (far_gain, gain), (far_taps, taps), (w_out, w_here))
        )
    ]
    late = []
    for s in range(8):
        row = pl.multiple_of(slot_block(s) * CH, 64)
        late.append(
            pltpu.make_async_copy(
                w_in.at[pl.ds(row, 128), :], w_slot.at[pl.ds(128 * s, 128), :], sems.at[5 + 2 * s]
            )
        )
        row = pl.multiple_of(slot_block(s) * CH + 128, 64)
        late.append(
            pltpu.make_async_copy(
                w_in.at[pl.ds(row, 64), :],
                w_slot.at[pl.ds(MAIN + 64 * s, 64), :],
                sems.at[6 + 2 * s],
            )
        )
    for copy in near + late:
        copy.start()
    near[0].wait()
    near[1].wait()
    for j in range(12):
        at = slice(128 * j, 128 * j + 128)
        mixed[:, at] = (cot[:, at].astype(F32) * scale[j : j + 1, :]).astype(BF16)
    near[2].wait()
    near[3].wait()
    for a in range(7):
        rows = slice(7 * a, 7 * a + 7)
        taps_out[rows, :128] = taps[a, :, :128]
        taps_out[rows, 128:192] = taps[a, :, 128:]
        taps_out[rows, 192:] = taps[a, :, 128:]

    def unit(index, high):
        line = gain[pl.ds(index // 2, 1), :]
        return jnp.where(index % 2 == high, line, swap(line))

    low = lanes((1, 128)) < 64
    rest = []
    for s in range(8):
        u = 3 * slot_block(s)
        main = jnp.where(low, unit(u, 0), unit(u + 1, 1))
        gain_slot[:, 128 * s : 128 * s + 128] = main
        rest.append(unit(u + 2, s % 2))
        if s == 0:
            gain_own[0:1, :] = main
            gain_own[1:2, :] = jnp.where(low, rest[0], swap(rest[0]))
    for t in range(4):
        at = MAIN + 128 * t
        gain_slot[:, at : at + 128] = jnp.where(low, rest[2 * t], rest[2 * t + 1])

    def column(index, high):
        at = pl.multiple_of((index // 2) * 128, 128)
        tile = cot[:, pl.ds(at, 128)].astype(F32)
        return jnp.where(index % 2 == high, tile, swap(tile))

    u = 3 * my_block()
    low = lanes((PIX, 128)) < 64
    cot_own[:, :128] = jnp.where(low, column(u, 0), column(u + 1, 1)).astype(BF16)
    cot_own[:, 128:] = column(u + 2, 0).astype(BF16)
    near[4].wait()
    activ_grad[...] = lax.dot_general(
        mixed[...], w_here[...], (((1,), (1,)), ((), ())), preferred_element_type=F32
    )
    for copy in late:
        copy.wait()


def gelu_pair(v):
    c = math.sqrt(2.0 / math.pi)
    square = v * v
    t = jnp.tanh(c * v * (1.0 + 0.044715 * square))
    half = 0.5 * (1.0 + t)
    slope = half + 0.5 * v * (1.0 - t * t) * (c * (1.0 + 3.0 * 0.044715 * square))
    return v * half, slope


def split_hi_lo(value):
    hi = value.astype(BF16).astype(F32)
    return hi, value - hi


def middle_kernel(*refs):
    slots = refs[:8]
    gain, w_slot, activ_grad = refs[8:11]
    normed, activ, grad_hidden, stats = refs[11:15]
    payloads = list(refs[15:19]) + [refs[19].at[x] for x in range(2)] + [refs[20].at[x] for x in range(2)]
    payloads = [payloads[n] for n in (0, 1, 4, 5, 2, 3, 6, 7)]
    x, first, second = refs[21:]
    low = lanes((HALF, 128)) < 64
    for s in range(8):
        x[:, 128 * s : 128 * s + 128] = slots[s][:PIX, :].astype(F32)
    for t in range(4):
        even = slots[2 * t][PIX:PACK, :].astype(F32)
        odd = slots[2 * t + 1][PIX:PACK, :].astype(F32)
        at = MAIN + 128 * t
        for i in range(ROWS):
            e = even[i * HALF : (i + 1) * HALF]
            o = odd[i * HALF : (i + 1) * HALF]
            x[i * COLS : i * COLS + HALF, at : at + 128] = jnp.where(low, e, swap(o))
            x[i * COLS + HALF : (i + 1) * COLS, at : at + 128] = jnp.where(low, swap(e), o)
    low = lanes((GRP, 128)) < 64
    for start in range(0, PIX, GRP):
        rows = slice(start, start + GRP)
        values = x[rows, :]
        mean = jnp.sum(values, axis=1, keepdims=True) * (1.0 / CALL)
        centred = values - mean
        var = jnp.sum(centred * centred, axis=1, keepdims=True) * (1.0 / CALL)
        rstd = 1.0 / jnp.sqrt(var + 1e-06)
        nhat = centred * rstd
        x[rows, :] = nhat
        normed[rows, :] = (nhat * gain[...]).astype(BF16)
        stats[rows, :] = jnp.where(
            low, jnp.broadcast_to(mean, (GRP, 128)), jnp.broadcast_to(rstd, (GRP, 128))
        )
    for n in range(0, FF, 256):
        hidden = jnp.dot(normed[...], w_slot[:, n : n + 256], preferred_element_type=F32)
        value, slope = gelu_pair(hidden)
        activ[:, n : n + 256] = value.astype(BF16)
        grad_hidden[:, n : n + 256] = (activ_grad[:, n : n + 256] * slope).astype(BF16)
    low = lanes((HALF, 128)) < 64
    for t in range(4):
        for at, kind in ((256 * t, 0), (MAIN + 128 * t, 1)):
            width = 128 if kind else 256
            part = lax.dot_general(
                grad_hidden[...],
                w_slot[at : at + width, :],
                (((1,), (1,)), ((), ())),
                preferred_element_type=F32,
            )
            scaled = part * gain[:, at : at + width]
            cross = scaled * x[:, at : at + width]
            if kind == 0:
                scaled = scaled[:, :128] + scaled[:, 128:]
                cross = cross[:, :128] + cross[:, 128:]
                payloads[2 * t][:PIX, :] = part[:, :128].astype(BF16)
                payloads[2 * t + 1][:PIX, :] = part[:, 128:].astype(BF16)
            else:
                evens, odds = [], []
                for i in range(ROWS):
                    l = part[i * COLS : i * COLS + HALF]
                    r = part[i * COLS + HALF : (i + 1) * COLS]
                    evens.append(jnp.where(low, l, swap(r)))
                    odds.append(jnp.where(low, swap(l), r))
                tail = [jnp.zeros((PACK - PIX - REM, 128), F32)]
                payloads[2 * t][PIX:PACK, :] = jnp.concatenate(evens + tail).astype(BF16)
                payloads[2 * t + 1][PIX:PACK, :] = jnp.concatenate(odds + tail).astype(BF16)
            if t == 0 and kind == 0:
                first[...] = scaled
                second[...] = cross
            else:
                first[...] += scaled
                second[...] += cross
    lane = lanes((GRP, 128))
    moments = jnp.zeros((GRP, 128), F32)
    for g in range(PIX // GRP):
        rows = slice(g * GRP, (g + 1) * GRP)
        for q, ref in enumerate((first, second)):
            value = jnp.sum(ref[rows, :], axis=1, keepdims=True) * (1.0 / CALL)
            hi, lo = split_hi_lo(value)
            moments = jnp.where(lane == 32 * q + g, hi, moments)
            moments = jnp.where(lane == 32 * q + 16 + g, lo, moments)
    moments = moments.astype(BF16)
    for s in range(8):
        payloads[s][MOM:PAY, :] = moments


def sum_payloads(refs, o_ref):
    total = refs[0][...].astype(F32)
    for ref in refs[1:]:
        total = total + ref[...].astype(F32)
    o_ref[:MOM, :] = total[:MOM].astype(BF16)
    moments = total[MOM:]
    whole = moments + pltpu.roll(moments, 128 - 16, 1)
    hi, lo = split_hi_lo(whole)
    low = (lanes((GRP, 128)) & 31) < 16
    o_ref[MOM:, :] = jnp.where(low, hi, pltpu.roll(lo, 16, 1)).astype(BF16)


def far_sum_kernel(far, across, o_ref):
    sum_payloads((far, across), o_ref)


def other_sum_kernel(other, one, three, o_ref):
    sum_payloads((other, one.at[1], three.at[1]), o_ref)


def norm_back_kernel(a, b, c, d, e, conv, stats, gain, top, own, bot, o_ref, both_ref, terms, main_pad, rem_pad):
    total = a[...].astype(F32) + (b[...].astype(F32) + c[0].astype(F32)) + (d[0].astype(F32) + e[...].astype(F32))
    moments = total[MOM:]
    whole = moments + pltpu.roll(moments, 128 - 16, 1)
    firsts, seconds = [], []
    for g in range(PIX // GRP):
        firsts.append(jnp.broadcast_to(whole[:, g : g + 1], (GRP, 128)))
        seconds.append(jnp.broadcast_to(whole[:, 32 + g : 33 + g], (GRP, 128)))
    first = jnp.concatenate(firsts)
    second = jnp.concatenate(seconds)
    both = stats[...]
    low = lanes((PIX, 128)) < 64
    other = swap(both)
    mean = jnp.where(low, both, other)
    rstd = jnp.where(low, other, both)
    main = rstd * (
        total[:PIX] * gain[0:1, :] - first - (conv[:PIX, :].astype(F32) - mean) * rstd * second
    )
    o_ref[:PIX, :] = main.astype(BF16)
    low = lanes((HALF, 128)) < 64

    def folded(v):
        return jnp.concatenate(
            [
                jnp.where(low, v[i * COLS : i * COLS + HALF], v[i * COLS + HALF : (i + 1) * COLS])
                for i in range(ROWS)
            ]
        )

    mean, rstd, first, second = folded(mean), folded(rstd), folded(first), folded(second)
    crem = conv[PIX:PACK, :].astype(F32)[:REM]
    rem = rstd * (total[PIX : PIX + REM] * gain[1:2, :] - first - (crem - mean) * rstd * second)
    rem = jnp.concatenate([rem, jnp.zeros((PACK - PIX - REM, 128), F32)])
    o_ref[PIX:PACK, :] = rem.astype(BF16)
    kernel_terms(o_ref, top, own, bot, terms, main_pad, rem_pad)
    both_ref[:PACK, :] = o_ref[...]
    both_ref[PACK:, :] = terms[...].astype(BF16)


def put(own, keep, send, z, xlo, zero, one):
    zero, one = zero.astype(BF16), one.astype(BF16)
    keep[z, xlo, :, :] = jnp.where(own, zero, one)
    send[z, xlo, :, :] = jnp.where(own, one, zero)


def product(left, right):
    return lax.dot_general(left, right, (((0,), (0,)), ((), ())), preferred_element_type=F32)


def weights_out_kernel(activ, mixed, keep, send):
    own = my_core() == 0
    for t in range(4):
        part = product(mixed[:, 384 * t : 384 * t + 384], activ[...])
        for n in range(2):
            p = part[192 * n : 192 * n + 192]
            put(own, keep, send, 2 * t + n, 0, p[0:48], p[48:96])
            put(own, keep, send, 2 * t + n, 1, p[96:144], p[144:192])


def weights_in_kernel(normed, grad_hidden, keep, send):
    own = my_core() == 0
    for t in range(4):
        part = product(normed[:, 256 * t : 256 * t + 256], grad_hidden[...])
        rest = product(normed[:, MAIN + 128 * t : MAIN + 128 * t + 128], grad_hidden[...])
        for n in range(2):
            p = part[128 * n : 128 * n + 128]
            q = rest[64 * n : 64 * n + 64]
            z = slot_block(2 * t + n)
            put(own, keep, send, z, 0, p[0:48], p[48:96])
            put(own, keep, send, z, 1, jnp.concatenate([p[96:128], q[0:16]]), q[16:64])


HALVES = ((0, 3, 4, 7), (1, 2, 5, 6))
PAIRS = (((0, 1), (2, 3)), ((0, 3), (1, 2)))


def kind_of(z):
    return 0 if z in HALVES[0] else 1


def pair_of(z):
    kind = kind_of(z)
    return next(q for q in range(2) if HALVES[kind].index(z) in PAIRS[kind][q])


def second_partner(z):
    return (z + (1 if z % 2 else -1)) % 8


def third_partner(z):
    half = HALVES[kind_of(z)]
    pair = [half[place] for place in PAIRS[kind_of(z)][pair_of(z)]]
    return pair[1 - pair.index(z)]


def by_z(table):
    z = lax.axis_index("rows") // 4
    value = 0
    for n, entry in enumerate(table):
        value = jnp.where(z == n, entry, value)
    return value


def added(a, b):
    return (a.astype(F32) + b.astype(F32)).astype(BF16)


def half_blocks(n):
    mine = by_z([HALVES[kind_of(z)][n] for z in range(8)])
    theirs = by_z([HALVES[1 - kind_of(z)][n] for z in range(8)])
    return mine, theirs


def join_half_kernel(keep, got, keep_next, send_next):
    for n in range(4):
        mine, theirs = half_blocks(n)
        keep_next[n] = added(keep[mine], got[mine])
        send_next[n] = added(keep[theirs], got[theirs])


def turned(z, turn):
    return (z - turn) % 8


def join_half_kernel(turn, keep, got, keep_next, send_next):
    for n in range(4):
        kinds = [kind_of(turned(z, turn)) for z in range(8)]
        mine = by_z([(HALVES[kind][n] + turn) % 8 for kind in kinds])
        theirs = by_z([(HALVES[1 - kind][n] + turn) % 8 for kind in kinds])
        keep_next[n] = added(keep[mine], got[mine])
        send_next[n] = added(keep[theirs], got[theirs])


def join_pair_kernel(turn, keep, got, keep_next, send_next):
    for n in range(2):
        places = [turned(z, turn) for z in range(8)]
        mine = by_z([PAIRS[kind_of(z)][pair_of(z)][n] for z in places])
        theirs = by_z([PAIRS[kind_of(z)][1 - pair_of(z)][n] for z in places])
        keep_next[n] = added(keep[mine], got[mine])
        send_next[n] = added(keep[theirs], got[theirs])


def join_lo_kernel(keep, got, keep_next, send_next):
    lo = my_lo()
    for n in range(keep.shape[0]):
        keep_next[n] = added(keep[n, lo], got[n, lo])
        send_next[n] = added(keep[n, 1 - lo], got[n, 1 - lo])


def put_terms(o_ref, at, total):
    for j in range(6):
        o_ref[at : at + 16, 128 * j : 128 * j + 128] = total[16 * j : 16 * j + 16]


def take_terms(ref, at):
    return jnp.concatenate(
        [ref[at : at + 16, 128 * j : 128 * j + 128].astype(F32) for j in range(6)], axis=0
    )


def own_place(turn):
    places = [turned(z, turn) for z in range(8)]
    return by_z([PAIRS[kind_of(z)][pair_of(z)].index(HALVES[kind_of(z)].index(z)) for z in places])


def join_one_in_kernel(keep, got, keep_next, send_next):
    own = own_place(1)
    keep_next[...] = added(keep[own], got[own])
    send_next[...] = added(keep[1 - own], got[1 - own])


def join_one_out_kernel(keep, got, terms, got_terms, keep_next, send_next):
    own = own_place(0)
    keep_next[...] = added(keep[own], got[own])
    send_next[:48, :] = added(keep[1 - own], got[1 - own])
    put_terms(send_next, 48, (terms[...] + got_terms[...]).astype(BF16))


def pass_kernel(terms, got, block, o_ref, block_ref):
    o_ref[...] = terms[...] + got[...]
    block_ref[...] = block[...]


def open_kernel(sent, got, o_ref):
    o_ref[...] = sent[PACK:, :].astype(F32) + got[PACK:, :].astype(F32)


def last_kernel(scale, keep_in, got_in, keep_out, sent, got, grad_in, grad_out, grad_kernel):
    grad_in[...] = (keep_in[...].astype(F32) + got_in[...].astype(F32)) * scale
    grad_out[...] = (keep_out[...].astype(F32) + got[:48, :].astype(F32)) * scale
    lines = (take_terms(sent, 48) + take_terms(got, 48)) * scale
    rest = jnp.concatenate([lines[64:89], swap(lines[64:96])[:24]], axis=0)
    for a in range(7):
        grad_kernel[a, :, :128] = lines[7 * a : 7 * a + 7]
        grad_kernel[a, :, 128:] = rest[7 * a : 7 * a + 7, :64]


def call(kernel, outs, args, scratch=(), mib=16, far=(), after=(), flops=0, moved=0):
    count = len(args)
    args = list(args) + list(after)

    def body(*refs):
        kernel(*refs[:count], *refs[len(args) :])

    near = pl.BlockSpec(memory_space=pltpu.VMEM)
    args = [pltpu.with_memory_space_constraint(a, pltpu.HBM) if n in far else a for n, a in enumerate(args)]
    hbm = pl.BlockSpec(memory_space=pltpu.HBM)
    single = not isinstance(outs, (list, tuple))
    shapes = [outs] if single else list(outs)
    result = pl.pallas_call(
        body,
        out_shape=shapes,
        in_specs=[hbm if n in far else near for n in range(len(args))],
        out_specs=[near] * len(shapes),
        scratch_shapes=list(scratch),
        compiler_params=limit(mib),
        cost_estimate=pl.CostEstimate(flops=flops, bytes_accessed=moved, transcendentals=0),
    )(*args)
    return result[0] if single else result


def shape(dims, dtype):
    return jax.ShapeDtypeStruct(dims, dtype)


def pads():
    return [pltpu.VMEM((9, COLS + 16, 128), F32), pltpu.VMEM((9, HALF + 16, 128), F32)]


def rows_perm(f):
    return [(i, f(i)) for i in range(32)]


def chan_shift(k, x):
    return [(i, ((i // 2 + k) % 4) * 2 + ((i % 2) ^ x)) for i in range(8)]


def other_side(block):
    return lax.ppermute(block, "rows", other_neighbour())


def shards(feature, kernel, ln_gain, layer_scale, w_in, w_out, cotangent):
    scale = 1.0 / math.sqrt(32 * PIX)
    slots = [(k, x) for k in range(4) for x in range(2)]

    packed = call(
        pack_kernel,
        shape((PACK, 128), BF16),
        [feature],
        [pltpu.VMEM((ROWS, COLS, CH), BF16), pltpu.SemaphoreType.DMA((1,))],
        far=(0,),
    )
    core = rows_perm(lambda i: i ^ 1)
    above, below = lax.ppermute(packed, "rows", core), other_side(packed)
    mixed, activ_grad, w_slot, gain_slot, gain_own, taps, cot_own = call(
        first_kernel,
        [
            shape((PIX, CALL), BF16),
            shape((PIX, FF), F32),
            shape((CALL, FF), BF16),
            shape((1, CALL), F32),
            shape((2, 128), F32),
            shape((49, 256), F32),
            shape((PIX, 256), BF16),
        ],
        [
            cotangent.reshape(PIX, CALL),
            layer_scale.reshape(12, 128),
            ln_gain.reshape(12, 128),
            kernel,
            w_out,
            w_in,
        ],
        [
            pltpu.VMEM((PIX, CALL), BF16),
            pltpu.VMEM((12, 128), F32),
            pltpu.VMEM((12, 128), F32),
            pltpu.VMEM((7, 7, CH), F32),
            pltpu.VMEM((FF, CALL), BF16),
            pltpu.SemaphoreType.DMA((21,)),
        ],
        far=range(6),
        flops=2 * PIX * CALL * FF,
        moved=8 << 20,
    )

    conv = call(
        conv_kernel, shape((PACK, 128), BF16), [above, packed, below, taps], pads(), flops=1 << 23, moved=1 << 20
    )

    def shift(block, k, x):
        return lax.ppermute(block, "chan", chan_shift(k, x))

    partner = shift(conv, 0, 1)
    gathered = {(0, 0): conv, (0, 1): partner}
    for k in (2, 1, 3):
        gathered[(4 - k) % 4, 0] = shift(conv, k, 0)
    for k in (1, 3):
        gathered[(4 - k) % 4, 1] = shift(partner, k, 0)
    gathered[2, 1] = shift(gathered[2, 0], 0, 1)

    outs = call(
        middle_kernel,
        [
            shape((PIX, CALL), BF16),
            shape((PIX, FF), BF16),
            shape((PIX, FF), BF16),
            shape((PIX, 128), F32),
        ]
        + [shape((PAY, 128), BF16)] * 4
        + [shape((2, PAY, 128), BF16)] * 2,
        [gathered[s] for s in slots] + [gain_slot, w_slot, activ_grad],
        [pltpu.VMEM((PIX, CALL), F32), pltpu.VMEM((PIX, 128), F32), pltpu.VMEM((PIX, 128), F32)],
        mib=16,
        flops=4 * PIX * CALL * FF,
        moved=8 << 20,
    )
    normed, activ, grad_hidden, stats = outs[:4]
    payload = dict(zip(((0, 0), (0, 1), (2, 0), (2, 1), 1, 3), outs[4:]))

    across = shift(payload[2, 1], 0, 1)
    far_sum = call(
        far_sum_kernel, shape((PAY, 128), BF16), [payload[2, 0], across], flops=COST_FAR, moved=1 << 20
    )
    beside = [shift(payload[k], k, 0) for k in (1, 3)]
    other_sum = call(
        other_sum_kernel,
        shape((PAY, 128), BF16),
        [payload[0, 1]] + beside,
        flops=COST_SUMS,
        moved=1 << 20,
    )
    crossed = shift(other_sum, 0, 1)
    mine = [shift(far_sum, 2, 0)] + beside

    pairs = [shape((8, 2, 48, FF), BF16)] * 2
    keep_out, send_out = call(
        weights_out_kernel, pairs, [activ, mixed], flops=COST_OUT, moved=8 << 20
    )
    got_out = lax.ppermute(send_out, "rows", core)
    keep_in, send_in = call(
        weights_in_kernel, pairs, [normed, grad_hidden], after=[other_sum, far_sum], flops=COST_IN, moved=8 << 20
    )
    got_in = lax.ppermute(send_in, "rows", core)
    def move(block, f):
        return lax.ppermute(block, "rows", rows_perm(f))

    def blocks(*dims):
        return shape(dims + (48, FF), BF16)

    def to_z(f):
        return lambda i: 4 * f(i // 4) + i % 4

    def to_lo(i):
        return i ^ 2

    def exchange(joiner, keep, got, dims, f, moved, after=()):
        keep, send = call(joiner, [blocks(*dims)] * 2, [keep, got], after=after, moved=moved)
        return keep, move(send, f)

    def first(z):
        return z ^ 1

    def half(turn):
        return lambda *refs: join_half_kernel(turn, *refs)

    def pair(turn):
        return lambda *refs: join_pair_kernel(turn, *refs)

    keep_out, got_out = exchange(half(0), keep_out, got_out, (4, 2), to_z(first), 4 << 20, [other_sum])
    keep_in, got_in = exchange(
        half(1), keep_in, got_in, (4, 2), to_z(second_partner), 4 << 20, [other_sum]
    )
    grad_conv, sent, terms = call(
        norm_back_kernel,
        [shape((PACK, 128), BF16), shape((PACK + TERMS, 128), BF16), shape((TERMS, 128), F32)],
        [payload[0, 0]] + mine + [crossed, conv, stats, gain_own, above, packed, below],
        pads(),
        flops=COST_BACK,
        moved=2 << 20,
    )

    def partner_terms(terms, f):
        return lax.ppermute(terms, "rows", rows_perm(f))

    grad_side = other_side(grad_conv)
    grad_core = lax.ppermute(sent, "rows", core)
    terms = call(open_kernel, shape((TERMS, 128), F32), [sent, grad_core])
    terms = terms + partner_terms(terms, to_lo)
    keep_out, got_out = exchange(
        pair(0), keep_out, got_out, (2, 2), to_z(second_partner), 2 << 20, [terms]
    )
    keep_in, got_in = exchange(join_lo_kernel, keep_in, got_in, (4,), to_lo, 2 << 20, [grad_side])
    terms, grad_side = call(
        pass_kernel,
        [shape((TERMS, 128), F32), shape((PACK, 128), BF16)],
        [terms, partner_terms(terms, to_z(first)), grad_side],
        moved=1 << 20,
    )
    keep_out, got_out = exchange(join_lo_kernel, keep_out, got_out, (2,), to_lo, 1 << 20, [terms])
    keep_in, got_in = exchange(pair(1), keep_in, got_in, (2,), to_z(first), 1 << 20, [terms])

    grad_feature = call(
        back_kernel,
        shape((ROWS, COLS, CH), BF16),
        [grad_core, grad_conv, grad_side, taps, cot_own],
        pads(),
        flops=1 << 23,
        moved=1 << 20,
    )
    keep_out, sent = call(
        join_one_out_kernel,
        [shape((48, FF), BF16), shape((64, FF), BF16)],
        [keep_out, got_out, terms, partner_terms(terms, to_z(second_partner))],
        moved=1 << 20,
    )
    got = move(sent, to_z(third_partner))
    keep_in, sent_in = call(
        join_one_in_kernel, [shape((48, FF), BF16)] * 2, [keep_in, got_in], moved=1 << 20
    )
    got_in = move(sent_in, to_z(lambda z: (third_partner((z - 1) % 8) + 1) % 8))
    grad_in, grad_out, grad_kernel = call(
        lambda *refs: last_kernel(scale, *refs),
        [shape((48, FF), F32), shape((48, FF), F32), shape((7, 7, CH), F32)],
        [keep_in, got_in, keep_out, sent, got],
        moved=1 << 20,
    )
    return grad_feature, grad_in, grad_out.T, grad_kernel


def solution(mesh):
    placed = (
        P("rows", None, "chan"),
        P(None, None, "chan"),
        P(),
        P(),
        P(None, "chan"),
        P("chan", None),
        P("rows", None, None),
    )
    return jax.shard_map(
        shards,
        mesh=mesh,
        in_specs=placed,
        out_specs=(
            P("rows", None, "chan"),
            P("rows", "chan"),
            P("chan", "rows"),
            P(None, None, "chan"),
        ),
        check_vma=False,
    )
```

```python
import math

import jax
import jax.numpy as jnp
from jax import lax
from jax.experimental import pallas as pl
from jax.experimental.pallas import tpu as pltpu
from jax.sharding import PartitionSpec as P

F32 = jnp.float32
BF16 = jnp.bfloat16

ROWS = 3
COLS = 144
PIX = ROWS * COLS
HALF = COLS // 2
CH = 192
REM = ROWS * HALF
PACK = 656
MOM = 656
PAY = 704
TERMS = 96
COST_BACK = 1 << 35
COST_OUT = 1 << 30
COST_PASS = 1 << 20
COST_FAR = 1 << 20
COST_IN = 1 << 30
COST_SUMS = 1 << 34
GRP = 48
CALL = 1536
FF = 768
MAIN = 1024


def lanes(shape):
    return lax.broadcasted_iota(jnp.int32, shape, len(shape) - 1)


def swap(x):
    return pltpu.roll(x, 64, x.ndim - 1)


def limit(mib):
    return pltpu.CompilerParams(vmem_limit_bytes=mib * 1024 * 1024)


def my_block():
    return lax.axis_index("chan")


def slot_block(s):
    me = my_block()
    return ((me // 2 + s // 2) % 4) * 2 + (me % 2 + s % 2) % 2


def my_core():
    return lax.axis_index("rows") % 2


def other_neighbour():
    pairs = [(i, i + 1) for i in range(1, 31, 2)]
    return pairs + [(b, a) for a, b in pairs]


def my_lo():
    return (lax.axis_index("rows") // 2) % 2


def pack_kernel(far, o_ref, x_ref, sem):
    copy = pltpu.make_async_copy(far, x_ref, sem.at[0])
    copy.start()
    copy.wait()
    parts = []
    low = lanes((HALF, 128)) < 64
    for i in range(ROWS):
        row = x_ref[i].astype(F32)
        o_ref[i * COLS : (i + 1) * COLS, :] = row[:, :128].astype(BF16)
        rem = jnp.concatenate([row[:, 128:], row[:, 128:]], axis=1)
        parts.append(jnp.where(low, rem[:HALF], rem[HALF:]))
    parts.append(jnp.zeros((PACK - PIX - REM, 128), F32))
    o_ref[PIX:PACK, :] = jnp.concatenate(parts, axis=0).astype(BF16)


def fill_pads(blocks, main_pad, rem_pad):
    low = lanes((8, 128)) < 64
    odd = my_core() == 1
    core, own, other = blocks

    def either(a, b, rows):
        return jnp.where(odd, a[rows, :].astype(F32), b[rows, :].astype(F32))

    whole, tail = slice(0, PIX), slice(PIX, PACK)
    parts = (
        (either(core, other, whole), either(core, other, tail)),
        (own[whole, :].astype(F32), own[tail, :].astype(F32)),
        (either(other, core, whole), either(other, core, tail)),
    )
    for n, (main, rem) in enumerate(parts):
        for i in range(ROWS):
            r = n * ROWS + i
            main_pad[r, 0:8, :] = jnp.zeros((8, 128), F32)
            main_pad[r, 8 : 8 + COLS, :] = main[i * COLS : (i + 1) * COLS]
            main_pad[r, 8 + COLS : 16 + COLS, :] = jnp.zeros((8, 128), F32)
            part = rem[i * HALF : (i + 1) * HALF]
            rem_pad[r, 8 : 8 + HALF, :] = part
            rem_pad[r, 0:8, :] = jnp.where(low, 0.0, swap(part[HALF - 8 :]))
            rem_pad[r, 8 + HALF : 16 + HALF, :] = jnp.where(low, swap(part[:8]), 0.0)


def taps_block(pad, k_ref, lane0, start, count, flip):
    acc = [None] * ROWS
    for b in range(7):
        for r in range(9):
            window = pad[r, start + 5 + b : start + 5 + b + count, :]
            for i in range(ROWS):
                a = r - i
                if 0 <= a <= 6:
                    tap = (6 - a) * 7 + (6 - b) if flip else a * 7 + b
                    term = window * k_ref[tap : tap + 1, lane0 : lane0 + 128]
                    acc[i] = term if acc[i] is None else acc[i] + term
    return acc


def conv_kernel(top, own, bot, k_ref, o_ref, main_pad, rem_pad):
    fill_pads((top, own, bot), main_pad, rem_pad)
    for start in range(0, COLS, 48):
        acc = taps_block(main_pad, k_ref, 0, start, 48, False)
        for i in range(ROWS):
            o_ref[i * COLS + start : i * COLS + start + 48, :] = acc[i].astype(BF16)
    parts = [[] for _ in range(ROWS)]
    for start in range(0, HALF, 24):
        acc = taps_block(rem_pad, k_ref, 128, start, 24, False)
        for i in range(ROWS):
            parts[i].append(acc[i])
    flat = [p for row in parts for p in row] + [jnp.zeros((PACK - PIX - REM, 128), F32)]
    o_ref[PIX:PACK, :] = jnp.concatenate(flat, axis=0).astype(BF16)


def back_kernel(top, own, bot, k_ref, cot_ref, o_ref, main_pad, rem_pad):
    fill_pads((top, own, bot), main_pad, rem_pad)
    for start in range(0, COLS, 48):
        acc = taps_block(main_pad, k_ref, 0, start, 48, True)
        for i in range(ROWS):
            cot = cot_ref[i * COLS + start : i * COLS + start + 48, :128].astype(F32)
            o_ref[i, start : start + 48, :128] = (acc[i] + cot).astype(BF16)
    parts = [[] for _ in range(ROWS)]
    for start in range(0, HALF, 24):
        acc = taps_block(rem_pad, k_ref, 128, start, 24, True)
        for i in range(ROWS):
            parts[i].append(acc[i])
    for i in range(ROWS):
        rem = jnp.concatenate(parts[i], axis=0)
        both = jnp.concatenate([rem[:, :64], swap(rem)[:, :64]], axis=0)
        cot = cot_ref[i * COLS : (i + 1) * COLS, 128:192].astype(F32)
        o_ref[i, :, 128:] = (both + cot).astype(BF16)


def kernel_terms(grad, top, own, bot, o_ref, main_pad, rem_pad):
    fill_pads((top, own, bot), main_pad, rem_pad)
    o_ref[...] = jnp.zeros((TERMS, 128), F32)
    gmain = grad[:PIX, :].astype(F32)
    grem = grad[PIX:PACK, :].astype(F32)
    for pad, part, width, folded in ((main_pad, gmain, COLS, False), (rem_pad, grem, HALF, True)):
        for b in range(7):
            acc = [jnp.zeros((8, 128), F32)] * 7
            for start in range(0, width, 8):
                windows = [pad[r, start + 5 + b : start + 13 + b, :] for r in range(9)]
                for i in range(ROWS):
                    g = part[i * width + start : i * width + start + 8]
                    for a in range(7):
                        acc[a] = acc[a] + g * windows[i + a]
            for a in range(7):
                total = jnp.sum(acc[a], axis=0, keepdims=True)
                t = a * 7 + b
                if not folded:
                    o_ref[t : t + 1, :] = total
                else:
                    total = total + swap(total)
                    if t < 25:
                        o_ref[64 + t : 65 + t, :64] = total[:, :64]
                    else:
                        o_ref[39 + t : 40 + t, 64:] = total[:, 64:]


def first_kernel(far_cot, far_scale, far_gain, far_taps, w_out, w_in, mixed, activ_grad, w_slot, gain_slot,
                 gain_own, taps_out, cot_own, cot, scale, gain, taps, w_here, sems):
    near = [
        pltpu.make_async_copy(src, dst, sems.at[n])
        for n, (src, dst) in enumerate(
            ((far_scale, scale), (far_cot, cot), (far_gain, gain), (far_taps, taps), (w_out, w_here))
        )
    ]
    late = []
    for s in range(8):
        row = pl.multiple_of(slot_block(s) * CH, 64)
        late.append(
            pltpu.make_async_copy(
                w_in.at[pl.ds(row, 128), :], w_slot.at[pl.ds(128 * s, 128), :], sems.at[5 + 2 * s]
            )
        )
        row = pl.multiple_of(slot_block(s) * CH + 128, 64)
        late.append(
            pltpu.make_async_copy(
                w_in.at[pl.ds(row, 64), :],
                w_slot.at[pl.ds(MAIN + 64 * s, 64), :],
                sems.at[6 + 2 * s],
            )
        )
    for copy in near + late:
        copy.start()
    near[0].wait()
    near[1].wait()
    for j in range(12):
        at = slice(128 * j, 128 * j + 128)
        mixed[:, at] = (cot[:, at].astype(F32) * scale[j : j + 1, :]).astype(BF16)
    near[2].wait()
    near[3].wait()
    for a in range(7):
        rows = slice(7 * a, 7 * a + 7)
        taps_out[rows, :128] = taps[a, :, :128]
        taps_out[rows, 128:192] = taps[a, :, 128:]
        taps_out[rows, 192:] = taps[a, :, 128:]

    def unit(index, high):
        line = gain[pl.ds(index // 2, 1), :]
        return jnp.where(index % 2 == high, line, swap(line))

    low = lanes((1, 128)) < 64
    rest = []
    for s in range(8):
        u = 3 * slot_block(s)
        main = jnp.where(low, unit(u, 0), unit(u + 1, 1))
        gain_slot[:, 128 * s : 128 * s + 128] = main
        rest.append(unit(u + 2, s % 2))
        if s == 0:
            gain_own[0:1, :] = main
            gain_own[1:2, :] = jnp.where(low, rest[0], swap(rest[0]))
    for t in range(4):
        at = MAIN + 128 * t
        gain_slot[:, at : at + 128] = jnp.where(low, rest[2 * t], rest[2 * t + 1])

    def column(index, high):
        at = pl.multiple_of((index // 2) * 128, 128)
        tile = cot[:, pl.ds(at, 128)].astype(F32)
        return jnp.where(index % 2 == high, tile, swap(tile))

    u = 3 * my_block()
    low = lanes((PIX, 128)) < 64
    cot_own[:, :128] = jnp.where(low, column(u, 0), column(u + 1, 1)).astype(BF16)
    cot_own[:, 128:] = column(u + 2, 0).astype(BF16)
    near[4].wait()
    activ_grad[...] = lax.dot_general(
        mixed[...], w_here[...], (((1,), (1,)), ((), ())), preferred_element_type=F32
    )
    for copy in late:
        copy.wait()


def gelu_pair(v):
    c = math.sqrt(2.0 / math.pi)
    square = v * v
    t = jnp.tanh(c * v * (1.0 + 0.044715 * square))
    half = 0.5 * (1.0 + t)
    slope = half + 0.5 * v * (1.0 - t * t) * (c * (1.0 + 3.0 * 0.044715 * square))
    return v * half, slope


def split_hi_lo(value):
    hi = value.astype(BF16).astype(F32)
    return hi, value - hi


def middle_kernel(*refs):
    slots = refs[:8]
    gain, w_slot, activ_grad = refs[8:11]
    normed, activ, grad_hidden, stats = refs[11:15]
    payloads = list(refs[15:19]) + [refs[19].at[x] for x in range(2)] + [refs[20].at[x] for x in range(2)]
    payloads = [payloads[n] for n in (0, 1, 4, 5, 2, 3, 6, 7)]
    x, first, second = refs[21:]
    low = lanes((HALF, 128)) < 64
    for s in range(8):
        x[:, 128 * s : 128 * s + 128] = slots[s][:PIX, :].astype(F32)
    for t in range(4):
        even = slots[2 * t][PIX:PACK, :].astype(F32)
        odd = slots[2 * t + 1][PIX:PACK, :].astype(F32)
        at = MAIN + 128 * t
        for i in range(ROWS):
            e = even[i * HALF : (i + 1) * HALF]
            o = odd[i * HALF : (i + 1) * HALF]
            x[i * COLS : i * COLS + HALF, at : at + 128] = jnp.where(low, e, swap(o))
            x[i * COLS + HALF : (i + 1) * COLS, at : at + 128] = jnp.where(low, swap(e), o)
    low = lanes((GRP, 128)) < 64
    for start in range(0, PIX, GRP):
        rows = slice(start, start + GRP)
        values = x[rows, :]
        mean = jnp.sum(values, axis=1, keepdims=True) * (1.0 / CALL)
        centred = values - mean
        var = jnp.sum(centred * centred, axis=1, keepdims=True) * (1.0 / CALL)
        rstd = 1.0 / jnp.sqrt(var + 1e-06)
        nhat = centred * rstd
        x[rows, :] = nhat
        normed[rows, :] = (nhat * gain[...]).astype(BF16)
        stats[rows, :] = jnp.where(
            low, jnp.broadcast_to(mean, (GRP, 128)), jnp.broadcast_to(rstd, (GRP, 128))
        )
    for n in range(0, FF, 256):
        hidden = jnp.dot(normed[...], w_slot[:, n : n + 256], preferred_element_type=F32)
        value, slope = gelu_pair(hidden)
        activ[:, n : n + 256] = value.astype(BF16)
        grad_hidden[:, n : n + 256] = (activ_grad[:, n : n + 256] * slope).astype(BF16)
    low = lanes((HALF, 128)) < 64
    for t in range(4):
        for at, kind in ((256 * t, 0), (MAIN + 128 * t, 1)):
            width = 128 if kind else 256
            part = lax.dot_general(
                grad_hidden[...],
                w_slot[at : at + width, :],
                (((1,), (1,)), ((), ())),
                preferred_element_type=F32,
            )
            scaled = part * gain[:, at : at + width]
            cross = scaled * x[:, at : at + width]
            if kind == 0:
                scaled = scaled[:, :128] + scaled[:, 128:]
                cross = cross[:, :128] + cross[:, 128:]
                payloads[2 * t][:PIX, :] = part[:, :128].astype(BF16)
                payloads[2 * t + 1][:PIX, :] = part[:, 128:].astype(BF16)
            else:
                evens, odds = [], []
                for i in range(ROWS):
                    l = part[i * COLS : i * COLS + HALF]
                    r = part[i * COLS + HALF : (i + 1) * COLS]
                    evens.append(jnp.where(low, l, swap(r)))
                    odds.append(jnp.where(low, swap(l), r))
                tail = [jnp.zeros((PACK - PIX - REM, 128), F32)]
                payloads[2 * t][PIX:PACK, :] = jnp.concatenate(evens + tail).astype(BF16)
                payloads[2 * t + 1][PIX:PACK, :] = jnp.concatenate(odds + tail).astype(BF16)
            if t == 0 and kind == 0:
                first[...] = scaled
                second[...] = cross
            else:
                first[...] += scaled
                second[...] += cross
    lane = lanes((GRP, 128))
    moments = jnp.zeros((GRP, 128), F32)
    for g in range(PIX // GRP):
        rows = slice(g * GRP, (g + 1) * GRP)
        for q, ref in enumerate((first, second)):
            value = jnp.sum(ref[rows, :], axis=1, keepdims=True) * (1.0 / CALL)
            hi, lo = split_hi_lo(value)
            moments = jnp.where(lane == 32 * q + g, hi, moments)
            moments = jnp.where(lane == 32 * q + 16 + g, lo, moments)
    moments = moments.astype(BF16)
    for s in range(8):
        payloads[s][MOM:PAY, :] = moments


def sum_payloads(refs, o_ref):
    total = refs[0][...].astype(F32)
    for ref in refs[1:]:
        total = total + ref[...].astype(F32)
    o_ref[:MOM, :] = total[:MOM].astype(BF16)
    moments = total[MOM:]
    whole = moments + pltpu.roll(moments, 128 - 16, 1)
    hi, lo = split_hi_lo(whole)
    low = (lanes((GRP, 128)) & 31) < 16
    o_ref[MOM:, :] = jnp.where(low, hi, pltpu.roll(lo, 16, 1)).astype(BF16)


def far_sum_kernel(far, across, o_ref):
    sum_payloads((far, across), o_ref)


def other_sum_kernel(other, one, three, o_ref):
    sum_payloads((other, one.at[1], three.at[1]), o_ref)


def norm_back_kernel(a, b, c, d, e, conv, stats, gain, top, own, bot, o_ref, both_ref, terms, main_pad, rem_pad):
    total = a[...].astype(F32) + (b[...].astype(F32) + c[0].astype(F32)) + (d[0].astype(F32) + e[...].astype(F32))
    moments = total[MOM:]
    whole = moments + pltpu.roll(moments, 128 - 16, 1)
    firsts, seconds = [], []
    for g in range(PIX // GRP):
        firsts.append(jnp.broadcast_to(whole[:, g : g + 1], (GRP, 128)))
        seconds.append(jnp.broadcast_to(whole[:, 32 + g : 33 + g], (GRP, 128)))
    first = jnp.concatenate(firsts)
    second = jnp.concatenate(seconds)
    both = stats[...]
    low = lanes((PIX, 128)) < 64
    other = swap(both)
    mean = jnp.where(low, both, other)
    rstd = jnp.where(low, other, both)
    main = rstd * (
        total[:PIX] * gain[0:1, :] - first - (conv[:PIX, :].astype(F32) - mean) * rstd * second
    )
    o_ref[:PIX, :] = main.astype(BF16)
    low = lanes((HALF, 128)) < 64

    def folded(v):
        return jnp.concatenate(
            [
                jnp.where(low, v[i * COLS : i * COLS + HALF], v[i * COLS + HALF : (i + 1) * COLS])
                for i in range(ROWS)
            ]
        )

    mean, rstd, first, second = folded(mean), folded(rstd), folded(first), folded(second)
    crem = conv[PIX:PACK, :].astype(F32)[:REM]
    rem = rstd * (total[PIX : PIX + REM] * gain[1:2, :] - first - (crem - mean) * rstd * second)
    rem = jnp.concatenate([rem, jnp.zeros((PACK - PIX - REM, 128), F32)])
    o_ref[PIX:PACK, :] = rem.astype(BF16)
    kernel_terms(o_ref, top, own, bot, terms, main_pad, rem_pad)
    both_ref[:PACK, :] = o_ref[...]
    both_ref[PACK:, :] = terms[...].astype(BF16)


def put(own, keep, send, z, xlo, zero, one):
    zero, one = zero.astype(BF16), one.astype(BF16)
    keep[z, xlo, :, :] = jnp.where(own, zero, one)
    send[z, xlo, :, :] = jnp.where(own, one, zero)


def product(left, right):
    return lax.dot_general(left, right, (((0,), (0,)), ((), ())), preferred_element_type=F32)


def weights_out_kernel(activ, mixed, keep, send):
    own = my_core() == 0
    for t in range(4):
        part = product(mixed[:, 384 * t : 384 * t + 384], activ[...])
        for n in range(2):
            p = part[192 * n : 192 * n + 192]
            put(own, keep, send, 2 * t + n, 0, p[0:48], p[48:96])
            put(own, keep, send, 2 * t + n, 1, p[96:144], p[144:192])


def weights_in_kernel(normed, grad_hidden, keep, send):
    own = my_core() == 0
    for t in range(4):
        part = product(normed[:, 256 * t : 256 * t + 256], grad_hidden[...])
        rest = product(normed[:, MAIN + 128 * t : MAIN + 128 * t + 128], grad_hidden[...])
        for n in range(2):
            p = part[128 * n : 128 * n + 128]
            q = rest[64 * n : 64 * n + 64]
            z = slot_block(2 * t + n)
            put(own, keep, send, z, 0, p[0:48], p[48:96])
            put(own, keep, send, z, 1, jnp.concatenate([p[96:128], q[0:16]]), q[16:64])


HALVES = ((0, 3, 4, 7), (1, 2, 5, 6))
PAIRS = (((0, 1), (2, 3)), ((0, 3), (1, 2)))


def kind_of(z):
    return 0 if z in HALVES[0] else 1


def pair_of(z):
    kind = kind_of(z)
    return next(q for q in range(2) if HALVES[kind].index(z) in PAIRS[kind][q])


def second_partner(z):
    return (z + (1 if z % 2 else -1)) % 8


def third_partner(z):
    half = HALVES[kind_of(z)]
    pair = [half[place] for place in PAIRS[kind_of(z)][pair_of(z)]]
    return pair[1 - pair.index(z)]


def by_z(table):
    z = lax.axis_index("rows") // 4
    value = 0
    for n, entry in enumerate(table):
        value = jnp.where(z == n, entry, value)
    return value


def added(a, b):
    return (a.astype(F32) + b.astype(F32)).astype(BF16)


def half_blocks(n):
    mine = by_z([HALVES[kind_of(z)][n] for z in range(8)])
    theirs = by_z([HALVES[1 - kind_of(z)][n] for z in range(8)])
    return mine, theirs


def join_half_kernel(keep, got, keep_next, send_next):
    for n in range(4):
        mine, theirs = half_blocks(n)
        keep_next[n] = added(keep[mine], got[mine])
        send_next[n] = added(keep[theirs], got[theirs])


def turned(z, turn):
    return (z - turn) % 8


def join_half_kernel(turn, keep, got, keep_next, send_next):
    for n in range(4):
        kinds = [kind_of(turned(z, turn)) for z in range(8)]
        mine = by_z([(HALVES[kind][n] + turn) % 8 for kind in kinds])
        theirs = by_z([(HALVES[1 - kind][n] + turn) % 8 for kind in kinds])
        keep_next[n] = added(keep[mine], got[mine])
        send_next[n] = added(keep[theirs], got[theirs])


def join_pair_kernel(turn, keep, got, keep_next, send_next):
    for n in range(2):
        places = [turned(z, turn) for z in range(8)]
        mine = by_z([PAIRS[kind_of(z)][pair_of(z)][n] for z in places])
        theirs = by_z([PAIRS[kind_of(z)][1 - pair_of(z)][n] for z in places])
        keep_next[n] = added(keep[mine], got[mine])
        send_next[n] = added(keep[theirs], got[theirs])


def join_lo_kernel(keep, got, keep_next, send_next):
    lo = my_lo()
    for n in range(keep.shape[0]):
        keep_next[n] = added(keep[n, lo], got[n, lo])
        send_next[n] = added(keep[n, 1 - lo], got[n, 1 - lo])


def put_terms(o_ref, at, total):
    for j in range(6):
        o_ref[at : at + 16, 128 * j : 128 * j + 128] = total[16 * j : 16 * j + 16]


def take_terms(ref, at):
    return jnp.concatenate(
        [ref[at : at + 16, 128 * j : 128 * j + 128].astype(F32) for j in range(6)], axis=0
    )


def own_place(turn):
    places = [turned(z, turn) for z in range(8)]
    return by_z([PAIRS[kind_of(z)][pair_of(z)].index(HALVES[kind_of(z)].index(z)) for z in places])


def join_one_in_kernel(keep, got, keep_next, send_next):
    own = own_place(1)
    keep_next[...] = added(keep[own], got[own])
    send_next[...] = added(keep[1 - own], got[1 - own])


def join_one_out_kernel(keep, got, terms, got_terms, keep_next, send_next):
    own = own_place(0)
    keep_next[...] = added(keep[own], got[own])
    send_next[:48, :] = added(keep[1 - own], got[1 - own])
    put_terms(send_next, 48, (terms[...] + got_terms[...]).astype(BF16))


def pass_kernel(terms, got, block, o_ref, block_ref):
    o_ref[...] = terms[...] + got[...]
    block_ref[...] = block[...]


def open_kernel(sent, got, o_ref):
    o_ref[...] = sent[PACK:, :].astype(F32) + got[PACK:, :].astype(F32)


def last_kernel(scale, keep_in, got_in, keep_out, sent, got, grad_in, grad_out, grad_kernel):
    grad_in[...] = (keep_in[...].astype(F32) + got_in[...].astype(F32)) * scale
    grad_out[...] = (keep_out[...].astype(F32) + got[:48, :].astype(F32)) * scale
    lines = (take_terms(sent, 48) + take_terms(got, 48)) * scale
    rest = jnp.concatenate([lines[64:89], swap(lines[64:96])[:24]], axis=0)
    for a in range(7):
        grad_kernel[a, :, :128] = lines[7 * a : 7 * a + 7]
        grad_kernel[a, :, 128:] = rest[7 * a : 7 * a + 7, :64]


def call(kernel, outs, args, scratch=(), mib=16, far=(), after=(), flops=0, moved=0):
    count = len(args)
    args = list(args) + list(after)

    def body(*refs):
        kernel(*refs[:count], *refs[len(args) :])

    near = pl.BlockSpec(memory_space=pltpu.VMEM)
    args = [pltpu.with_memory_space_constraint(a, pltpu.HBM) if n in far else a for n, a in enumerate(args)]
    hbm = pl.BlockSpec(memory_space=pltpu.HBM)
    single = not isinstance(outs, (list, tuple))
    shapes = [outs] if single else list(outs)
    result = pl.pallas_call(
        body,
        out_shape=shapes,
        in_specs=[hbm if n in far else near for n in range(len(args))],
        out_specs=[near] * len(shapes),
        scratch_shapes=list(scratch),
        compiler_params=limit(mib),
        cost_estimate=pl.CostEstimate(flops=flops, bytes_accessed=moved, transcendentals=0),
    )(*args)
    return result[0] if single else result


def shape(dims, dtype):
    return jax.ShapeDtypeStruct(dims, dtype)


def pads():
    return [pltpu.VMEM((9, COLS + 16, 128), F32), pltpu.VMEM((9, HALF + 16, 128), F32)]


def rows_perm(f):
    return [(i, f(i)) for i in range(32)]


def chan_shift(k, x):
    return [(i, ((i // 2 + k) % 4) * 2 + ((i % 2) ^ x)) for i in range(8)]


def other_side(block):
    return lax.ppermute(block, "rows", other_neighbour())


def shards(feature, kernel, ln_gain, layer_scale, w_in, w_out, cotangent):
    scale = 1.0 / math.sqrt(32 * PIX)
    slots = [(k, x) for k in range(4) for x in range(2)]

    packed = call(
        pack_kernel,
        shape((PACK, 128), BF16),
        [feature],
        [pltpu.VMEM((ROWS, COLS, CH), BF16), pltpu.SemaphoreType.DMA((1,))],
        far=(0,),
    )
    core = rows_perm(lambda i: i ^ 1)
    above, below = lax.ppermute(packed, "rows", core), other_side(packed)
    mixed, activ_grad, w_slot, gain_slot, gain_own, taps, cot_own = call(
        first_kernel,
        [
            shape((PIX, CALL), BF16),
            shape((PIX, FF), F32),
            shape((CALL, FF), BF16),
            shape((1, CALL), F32),
            shape((2, 128), F32),
            shape((49, 256), F32),
            shape((PIX, 256), BF16),
        ],
        [
            cotangent.reshape(PIX, CALL),
            layer_scale.reshape(12, 128),
            ln_gain.reshape(12, 128),
            kernel,
            w_out,
            w_in,
        ],
        [
            pltpu.VMEM((PIX, CALL), BF16),
            pltpu.VMEM((12, 128), F32),
            pltpu.VMEM((12, 128), F32),
            pltpu.VMEM((7, 7, CH), F32),
            pltpu.VMEM((FF, CALL), BF16),
            pltpu.SemaphoreType.DMA((21,)),
        ],
        far=range(6),
        flops=2 * PIX * CALL * FF,
        moved=8 << 20,
    )

    conv = call(
        conv_kernel, shape((PACK, 128), BF16), [above, packed, below, taps], pads(), flops=1 << 23, moved=1 << 20
    )

    def shift(block, k, x):
        return lax.ppermute(block, "chan", chan_shift(k, x))

    partner = shift(conv, 0, 1)
    gathered = {(0, 0): conv, (0, 1): partner}
    for k in (2, 1, 3):
        gathered[(4 - k) % 4, 0] = shift(conv, k, 0)
    for k in (1, 3):
        gathered[(4 - k) % 4, 1] = shift(partner, k, 0)
    gathered[2, 1] = shift(gathered[2, 0], 0, 1)

    outs = call(
        middle_kernel,
        [
            shape((PIX, CALL), BF16),
            shape((PIX, FF), BF16),
            shape((PIX, FF), BF16),
            shape((PIX, 128), F32),
        ]
        + [shape((PAY, 128), BF16)] * 4
        + [shape((2, PAY, 128), BF16)] * 2,
        [gathered[s] for s in slots] + [gain_slot, w_slot, activ_grad],
        [pltpu.VMEM((PIX, CALL), F32), pltpu.VMEM((PIX, 128), F32), pltpu.VMEM((PIX, 128), F32)],
        mib=16,
        flops=4 * PIX * CALL * FF,
        moved=8 << 20,
    )
    normed, activ, grad_hidden, stats = outs[:4]
    payload = dict(zip(((0, 0), (0, 1), (2, 0), (2, 1), 1, 3), outs[4:]))

    across = shift(payload[2, 1], 0, 1)
    far_sum = call(
        far_sum_kernel, shape((PAY, 128), BF16), [payload[2, 0], across], flops=COST_FAR, moved=1 << 20
    )
    beside = [shift(payload[k], k, 0) for k in (1, 3)]
    other_sum = call(
        other_sum_kernel,
        shape((PAY, 128), BF16),
        [payload[0, 1]] + beside,
        flops=COST_SUMS,
        moved=1 << 20,
    )
    crossed = shift(other_sum, 0, 1)
    mine = [shift(far_sum, 2, 0)] + beside

    pairs = [shape((8, 2, 48, FF), BF16)] * 2
    keep_out, send_out = call(
        weights_out_kernel, pairs, [activ, mixed], flops=COST_OUT, moved=8 << 20
    )
    got_out = lax.ppermute(send_out, "rows", core)
    keep_in, send_in = call(
        weights_in_kernel, pairs, [normed, grad_hidden], after=[across], flops=COST_IN, moved=8 << 20
    )
    got_in = lax.ppermute(send_in, "rows", core)
    def move(block, f):
        return lax.ppermute(block, "rows", rows_perm(f))

    def blocks(*dims):
        return shape(dims + (48, FF), BF16)

    def to_z(f):
        return lambda i: 4 * f(i // 4) + i % 4

    def to_lo(i):
        return i ^ 2

    def exchange(joiner, keep, got, dims, f, moved, after=()):
        keep, send = call(joiner, [blocks(*dims)] * 2, [keep, got], after=after, moved=moved)
        return keep, move(send, f)

    def first(z):
        return z ^ 1

    def half(turn):
        return lambda *refs: join_half_kernel(turn, *refs)

    def pair(turn):
        return lambda *refs: join_pair_kernel(turn, *refs)

    keep_out, got_out = exchange(half(0), keep_out, got_out, (4, 2), to_z(first), 4 << 20, [other_sum])
    keep_in, got_in = exchange(
        half(1), keep_in, got_in, (4, 2), to_z(second_partner), 4 << 20, [other_sum]
    )
    grad_conv, sent, terms = call(
        norm_back_kernel,
        [shape((PACK, 128), BF16), shape((PACK + TERMS, 128), BF16), shape((TERMS, 128), F32)],
        [payload[0, 0]] + mine + [crossed, conv, stats, gain_own, above, packed, below],
        pads(),
        flops=COST_BACK,
        moved=2 << 20,
    )

    def partner_terms(terms, f):
        return lax.ppermute(terms, "rows", rows_perm(f))

    grad_side = other_side(grad_conv)
    grad_core = lax.ppermute(sent, "rows", core)
    terms = call(open_kernel, shape((TERMS, 128), F32), [sent, grad_core])
    terms = terms + partner_terms(terms, to_lo)
    keep_out, got_out = exchange(
        pair(0), keep_out, got_out, (2, 2), to_z(second_partner), 2 << 20, [terms]
    )
    keep_in, got_in = exchange(join_lo_kernel, keep_in, got_in, (4,), to_lo, 2 << 20, [grad_side])
    terms, grad_side = call(
        pass_kernel,
        [shape((TERMS, 128), F32), shape((PACK, 128), BF16)],
        [terms, partner_terms(terms, to_z(first)), grad_side],
        moved=1 << 20,
    )
    keep_out, got_out = exchange(join_lo_kernel, keep_out, got_out, (2,), to_lo, 1 << 20, [terms])
    keep_in, got_in = exchange(pair(1), keep_in, got_in, (2,), to_z(first), 1 << 20, [terms])

    grad_feature = call(
        back_kernel,
        shape((ROWS, COLS, CH), BF16),
        [grad_core, grad_conv, grad_side, taps, cot_own],
        pads(),
        flops=1 << 23,
        moved=1 << 20,
    )
    keep_out, sent = call(
        join_one_out_kernel,
        [shape((48, FF), BF16), shape((64, FF), BF16)],
        [keep_out, got_out, terms, partner_terms(terms, to_z(second_partner))],
        moved=1 << 20,
    )
    got = move(sent, to_z(third_partner))
    keep_in, sent_in = call(
        join_one_in_kernel, [shape((48, FF), BF16)] * 2, [keep_in, got_in], moved=1 << 20
    )
    got_in = move(sent_in, to_z(lambda z: (third_partner((z - 1) % 8) + 1) % 8))
    grad_in, grad_out, grad_kernel = call(
        lambda *refs: last_kernel(scale, *refs),
        [shape((48, FF), F32), shape((48, FF), F32), shape((7, 7, CH), F32)],
        [keep_in, got_in, keep_out, sent, got],
        moved=1 << 20,
    )
    return grad_feature, grad_in, grad_out.T, grad_kernel


def solution(mesh):
    placed = (
        P("rows", None, "chan"),
        P(None, None, "chan"),
        P(),
        P(),
        P(None, "chan"),
        P("chan", None),
        P("rows", None, None),
    )
    return jax.shard_map(
        shards,
        mesh=mesh,
        in_specs=placed,
        out_specs=(
            P("rows", None, "chan"),
            P("rows", "chan"),
            P("chan", "rows"),
            P(None, None, "chan"),
        ),
        check_vma=False,
    )
```
